256 devices in a mesh: pool: 2 (over z_hi), grp: 16 (over z_lo, x), cuts: 8 (over y, core).
Axes of the slice: x: 4, y: 4, z: 8 (z_hi: 2, z_lo: 4; z = z_hi * 4 + z_lo), core: 2. Of those that a mesh axis runs over, the one named last changes fastest.
Arguments:
- residual_in: bfloat16 [1024, 6144], P(('pool', 'grp'), 'cuts'), may hold values from -64 to 64
- queries: bfloat16 [1024, 6144], P(('pool', 'grp'), 'cuts'), may hold values from -1024 to 1024
- key_new: bfloat16 [1024, 1024], P(('pool', 'grp'), 'cuts'), may hold values from -5 to 5
- value_new: bfloat16 [1024, 1024], P(('pool', 'grp'), 'cuts'), may hold values from -5 to 5
- key_cache: bfloat16 [1024, 128, 1024], P(('pool', 'grp'), None, 'cuts'), may hold values from -8 to 8
- value_cache: bfloat16 [1024, 128, 1024], P(('pool', 'grp'), None, 'cuts'), may hold values from -5 to 5
- cache_lens: int32 [1024], P(('pool', 'grp')), may hold values from 2 to 128, as said below
- norm_gain: float32 [6144], replicated, may hold values from 0.1 to 1.9
- expert_ids: int32 [1024, 4], P(('pool', 'grp')), may hold values from 0 to 15, all different within a row; in each aligned block of 32 rows (0 to 31, 32 to 63, ...) at most 16 rows name the same one
- gate_weights: float32 [1024, 4], P(('pool', 'grp')), may hold values from 0.1 to 0.6
- w_in: bfloat16 [16, 6144, 6144], P('grp', None, ('pool', 'cuts')), may hold values from -0.078125 to 0.078125
- w_out: bfloat16 [16, 6144, 6144], P('grp', ('pool', 'cuts')), may hold values from -0.078125 to 0.078125
Outputs:
- attended: bfloat16 [1024, 6144], P(('pool', 'grp'), 'cuts')
- expert_mix: bfloat16 [1024, 6144], P(('pool', 'grp'), 'cuts')
The draws below stay inside these ranges and needn't reach their ends.
Inputs may be any that keep to these rules, and one draw needn't show every extreme that they name: `expert_ids`: each row names 4 different experts; among the rows of one attention group (32 rows in order) no expert is named more than 16 times, a bound that some block reaches. `cache_lens`: the first row of every attention group has 128 live entries.
All inputs are finite; a program needn't handle non-finite values.
Results may differ from the reference program's by a relative error of at most 0.022.
Values may be sent and summed in bfloat16 or wider, within the bound.
A program may use at most 128 MiB of HBM per device.

```python
import math
import jax
import jax.numpy as jnp
import numpy as np
from jax import lax

D = 6144
Q_HEADS = 48
KV_HEADS = 8
HEAD_DIM = 128
FF_WIN = 6144
EXPERTS = 16
TOP = 4
R_DEV = 32
ROWS = 1024
LEN = 128
CAP = 16
N_POOL = 2
N_GRP = 16


def query_key_pair(key):
    base = jax.random.fold_in(key, 7)
    first_key, second_key, third_key = jax.random.split(base, 3)
    group_size = Q_HEADS // KV_HEADS
    keys = jnp.clip(jax.random.normal(first_key, (ROWS, LEN, KV_HEADS, HEAD_DIM), jnp.float32), -4.0, 4.0)
    position_scale = jax.random.uniform(second_key, (ROWS, LEN, KV_HEADS, 1), jnp.float32, 0.5, 1.5)
    position = jnp.arange(LEN)[None, :, None, None]
    position_scale = jnp.where(position < 2, 1.0, position_scale)
    keys = keys * position_scale
    query_vals = 0.5 * jnp.clip(jax.random.normal(third_key, (ROWS, KV_HEADS, group_size, HEAD_DIM), jnp.float32), -4.0, 4.0)
    return (query_vals.reshape(ROWS, D), keys.reshape(ROWS, LEN, KV_HEADS * HEAD_DIM))


def draw_queries(key, part):
    query_vals, keys = query_key_pair(key)
    return query_vals.astype(jnp.bfloat16)


def draw_key_cache(key, part):
    query_vals, keys = query_key_pair(key)
    return keys.astype(jnp.bfloat16)


def draw_cache_lens(key, part):
    key = jax.random.fold_in(key, 11)
    lengths = jax.random.randint(key, (ROWS,), 2, LEN + 1)
    leading_row = jnp.arange(ROWS) % R_DEV == 0
    return jnp.where(leading_row, LEN, lengths).astype(jnp.int32)


def draw_residual_in(key, part):
    key = jax.random.fold_in(key, 5)
    first_key = jax.random.fold_in(key, 0)
    third_key = jax.random.fold_in(key, 2)
    fourth_key = jax.random.fold_in(key, 3)
    row_scale = jnp.exp(jax.random.uniform(first_key, (ROWS, 1), jnp.float32, math.log(0.3), math.log(3.0)))
    col_scale = jnp.exp(jax.random.uniform(fourth_key, (1, D), jnp.float32, math.log(0.5), math.log(2.0)))
    entries = jnp.clip(jax.random.normal(third_key, (ROWS, D), jnp.float32), -4.0, 4.0)
    return (entries * row_scale * col_scale).astype(jnp.bfloat16)


def steps_of(key, shape, shards, low, top_value):
    gain, own = 1.0, jax.random.fold_in(key, 6)
    for axis_at, shards_of in shards:
        draws = jnp.exp(jax.random.uniform(jax.random.fold_in(own, axis_at), (shards_of,), jnp.float32, low / len(shards), top_value / len(shards)))
        gain = gain * jnp.repeat(draws, shape[axis_at] // shards_of).reshape([-1 if axis == axis_at else 1 for axis in range(len(shape))])
    return gain


def deal_out(rng, own, number, rows, amount, top, limit, lean):
    sequence = jax.random.permutation(rng, amount)
    heavy_load, ordinary = load_shares(amount, rows * top, limit, lean, True), load_shares(amount, rows * top, limit, lean, False)
    places = jnp.arange(amount)

    def named(sizes, turn):
        used = int((sizes > 0).sum())
        fixed = max(1, used // 4)
        shifted = fixed + (places - fixed + turn * (used - fixed)) % max(1, amount - fixed)
        return jnp.zeros((amount,), jnp.int32).at[sequence[jnp.where(places < fixed, places, shifted)]].set(jnp.asarray(sizes, jnp.int32))

    sizes = jnp.where(number % 4 == 0, named(heavy_load, number // 4), named(ordinary, number - number // 4 - 1))
    mixed = jax.random.permutation(jax.random.fold_in(own, 3), amount)
    donor, sink = mixed[0:amount // 2 * 2:2], mixed[1:amount // 2 * 2:2]
    room = jnp.minimum(sizes[donor] - 1, limit - sizes[sink]) // 2
    room = jnp.where((donor == sequence[0]) | (sink == sequence[0]) | (sizes[sink] == 0), 0, jnp.maximum(room, 0))
    shifted = jax.random.randint(jax.random.fold_in(own, 4), (amount // 2,), 0, 1 << 20) % (room + 1)
    sizes = sizes.at[donor].add(-shifted).at[sink].add(shifted)
    items = jnp.searchsorted(jnp.cumsum(sizes), jnp.arange(rows * top), side="right").astype(jnp.int32)
    listing = items.reshape(top, rows).T
    listing = listing[jax.random.permutation(jax.random.fold_in(own, 1), rows)]
    turn = jax.random.randint(jax.random.fold_in(own, 2), (rows, 1), 0, top)
    return jnp.take_along_axis(listing, (jnp.arange(top)[None, :] + turn) % top, axis=1)


def load_shares(amount, total, limit, skew, full):
    loads = [(1 << 20) // math.isqrt(grade ** skew) + 1 for grade in range(1, amount + 1)]
    largest = limit if full else min(limit, max(-(-total // amount), total * loads[0] // sum(loads)))
    least = 1 if total - largest >= amount - 1 else 0
    holding, surplus = [largest] + [least] * (amount - 1), total - largest - least * (amount - 1)
    while surplus > 0:
        free = [i for i in range(1, amount) if holding[i] < largest] or [i for i in range(1, amount) if holding[i] < limit]
        mass, budget = sum([loads[i] for i in free]), surplus
        for i in free:
            more = min(limit - holding[i], max(1, budget * loads[i] // mass), surplus)
            holding[i] = holding[i] + more
            surplus = surplus - more
    return np.array(holding)


def gaussian(stream_key, dims, width, most, cuts=(), kind=jnp.bfloat16):
    values = jax.random.normal(stream_key, dims, jnp.float32) * width
    if len(cuts) > 0:
        values = steps_of(stream_key, dims, cuts, -0.22, 0.18) * values
    return jnp.clip(values, min=-most, max=most).astype(kind)


def setup_inputs(seed: int = 0) -> dict:
    key_list = jax.random.split(jax.random.key(seed), 13)
    residual_in = draw_residual_in(jax.random.fold_in(key_list[12], 71), 0)
    queries = draw_queries(jax.random.fold_in(key_list[12], 71), 0)
    key_new = gaussian(key_list[2], (ROWS, KV_HEADS * HEAD_DIM), 1.0, 5.0, ((0, 32), (1, 8)))
    value_new = gaussian(key_list[3], (ROWS, KV_HEADS * HEAD_DIM), 1.0, 5.0, ((0, 32), (1, 8)))
    key_cache = draw_key_cache(jax.random.fold_in(key_list[12], 71), 0)
    value_cache = gaussian(key_list[5], (ROWS, LEN, KV_HEADS * HEAD_DIM), 1.0, 5.0, ((0, 32), (2, 8)))
    cache_lens = draw_cache_lens(jax.random.fold_in(key_list[12], 71), 0)
    norm_gain = jnp.clip(1.0 + 0.18 * jax.random.normal(key_list[7], (D,), jnp.float32), 0.1, 1.9)
    expert_ids_keys = jax.random.split(jax.random.fold_in(key_list[8], 1), ROWS // R_DEV)
    expert_ids_turns = jax.random.permutation(jax.random.fold_in(key_list[8], 3), ROWS // R_DEV)
    expert_ids = jax.vmap(lambda own, number: deal_out(jax.random.fold_in(key_list[8], 2), own, number, R_DEV, EXPERTS, TOP, CAP, 2))(expert_ids_keys, expert_ids_turns).reshape((ROWS, TOP))
    gate_weights = jnp.clip(0.1 + 0.5 * jax.random.uniform(key_list[9], (ROWS, TOP), jnp.float32) ** steps_of(key_list[9], (ROWS, TOP), ((0, 32),), -0.2, 0.2), 0.1, 0.6)
    w_in = gaussian(key_list[10], (EXPERTS, D, FF_WIN), D ** -0.5, 0.078125, ((0, 16), (2, 16)))
    w_out = gaussian(key_list[11], (EXPERTS, FF_WIN, D), FF_WIN ** -0.5, 0.078125, ((0, 16), (1, 16)))
    return {"residual_in": residual_in, "queries": queries, "key_new": key_new, "value_new": value_new, "key_cache": key_cache, "value_cache": value_cache, "cache_lens": cache_lens, "norm_gain": norm_gain, "expert_ids": expert_ids, "gate_weights": gate_weights, "w_in": w_in, "w_out": w_out}


def attend_block(queries, key_new, value_new, key_cache, value_cache, cache_lens):
    row_count = queries.shape[0]
    kv_count = key_cache.shape[-1] // HEAD_DIM
    group_size = queries.shape[-1] // key_cache.shape[-1]
    key_span = key_cache.shape[1]
    query_f = queries.astype(jnp.float32).reshape(row_count, kv_count, group_size, HEAD_DIM)
    keys_f = key_cache.astype(jnp.float32).reshape(row_count, key_span, kv_count, HEAD_DIM)
    values_f = value_cache.astype(jnp.float32).reshape(row_count, key_span, kv_count, HEAD_DIM)
    knew_f = key_new.astype(jnp.float32).reshape(row_count, kv_count, HEAD_DIM)
    vnew_f = value_new.astype(jnp.float32).reshape(row_count, kv_count, HEAD_DIM)
    score_scale = 1.0 / math.sqrt(HEAD_DIM)
    scores = jnp.einsum('rkgd,rtkd->rkgt', query_f, keys_f) * score_scale
    own_score = jnp.einsum('rkgd,rkd->rkg', query_f, knew_f) * score_scale
    live_mask = (jnp.arange(key_span, dtype=jnp.int32)[None, :] < cache_lens[:, None])[:, None, None, :]
    scores = jnp.where(live_mask, scores, -1e+30)
    row_peak = jnp.maximum(lax.optimization_barrier(jnp.max(scores, axis=-1)), own_score)
    raw_weights = jnp.where(live_mask, jnp.exp(scores - row_peak[..., None]), 0.0)
    own_weight = jnp.exp(own_score - row_peak)
    denominator = lax.optimization_barrier(jnp.sum(raw_weights, axis=-1)) + own_weight
    key_probs = (raw_weights / denominator[..., None]).astype(jnp.bfloat16)
    own_prob = (own_weight / denominator).astype(jnp.bfloat16)
    head_output = jnp.einsum('rkgt,rtkd->rkgd', key_probs.astype(jnp.float32), values_f)
    head_output = head_output + own_prob.astype(jnp.float32)[..., None] * vnew_f[:, :, None, :]
    return head_output.reshape(row_count, -1).astype(jnp.bfloat16)

def layer_norm(stream, norm_gain):
    stream_f = stream.astype(jnp.float32)
    mean_val = lax.optimization_barrier(jnp.mean(stream_f, axis=-1, keepdims=True))
    mean_sq = lax.optimization_barrier(jnp.mean(stream_f * stream_f, axis=-1, keepdims=True))
    variance = mean_sq - mean_val * mean_val
    return ((stream_f - mean_val) * lax.rsqrt(variance + 1e-05) * norm_gain).astype(jnp.bfloat16)

def reference(residual_in, queries, key_new, value_new, key_cache, value_cache, cache_lens, norm_gain, expert_ids, gate_weights, w_in, w_out):
    block_count = ROWS // R_DEV

    def per_block(packed):
        return attend_block(packed[0], packed[1], packed[2], packed[3], packed[4], packed[5])
    packed_all = (queries.reshape(block_count, R_DEV, -1), key_new.reshape(block_count, R_DEV, -1), value_new.reshape(block_count, R_DEV, -1), key_cache.reshape(block_count, R_DEV, LEN, -1), value_cache.reshape(block_count, R_DEV, LEN, -1), cache_lens.reshape(block_count, R_DEV))
    attended = lax.map(per_block, packed_all).reshape(ROWS, D)
    stream = (residual_in.astype(jnp.float32) + attended.astype(jnp.float32)).astype(jnp.bfloat16)
    normed = layer_norm(stream, norm_gain)
    slot_total = N_POOL * N_GRP * CAP

    def expert_step(carry, expert_index):
        matches = expert_ids == expert_index
        chosen = jnp.any(matches, axis=1)
        weight_col = lax.optimization_barrier(jnp.sum(jnp.where(matches, gate_weights, 0.0), axis=1))
        order = jnp.argsort(jnp.where(chosen, 0, 1).astype(jnp.int32), stable=True)[:slot_total]
        picked = normed[order]
        inner = jnp.dot(picked, w_in[expert_index], preferred_element_type=jnp.float32)
        hidden = jax.nn.silu(inner).astype(jnp.bfloat16)
        outcome = jnp.dot(hidden, w_out[expert_index], preferred_element_type=jnp.float32).astype(jnp.bfloat16)
        contrib = jnp.where(chosen[order][:, None], weight_col[order][:, None] * outcome.astype(jnp.float32), 0.0)
        return (carry.at[order].add(contrib), None)
    summed, unused = lax.scan(expert_step, jnp.zeros((ROWS, D), jnp.float32), jnp.arange(EXPERTS, dtype=jnp.int32))
    return (attended, summed.astype(jnp.bfloat16))
```

```python
import math

import jax
import jax.numpy as jnp
from jax import lax
from jax.experimental import pallas as pl
from jax.experimental.pallas import tpu as pltpu
from jax.sharding import PartitionSpec as P

HEAD_DIM = 128
MESH = pl.DeviceIdType.MESH
OFFS = (0, 1, 5, 7, 3, 2, 6, 4)
UNITS = 8
SLOTS = 16
CW = 768
CUTS = 8
FF = 384
D = CUTS * CW
ROWS = 32
GROUPS = 4
N_SEM = 160


def attend_local(queries, key_new, value_new, key_cache, value_cache, cache_lens):
    row_count = queries.shape[0]
    kv_count = key_cache.shape[-1] // HEAD_DIM
    group_size = queries.shape[-1] // key_cache.shape[-1]
    key_span = key_cache.shape[1]
    query_part = queries.reshape(row_count, kv_count, group_size, HEAD_DIM)
    keys_part = key_cache.reshape(row_count, key_span, kv_count, HEAD_DIM)
    values_part = value_cache.reshape(row_count, key_span, kv_count, HEAD_DIM)
    knew_part = key_new.reshape(row_count, kv_count, HEAD_DIM)
    vnew_f = value_new.astype(jnp.float32).reshape(row_count, kv_count, HEAD_DIM)
    score_scale = 1.0 / math.sqrt(HEAD_DIM)
    scores = (
        jnp.einsum("rkgd,rtkd->rkgt", query_part, keys_part, preferred_element_type=jnp.float32)
        * score_scale
    )
    own_score = (
        jnp.einsum("rkgd,rkd->rkg", query_part, knew_part, preferred_element_type=jnp.float32)
        * score_scale
    )
    live_mask = (jnp.arange(key_span, dtype=jnp.int32)[None, :] < cache_lens[:, None])[
        :, None, None, :
    ]
    scores = jnp.where(live_mask, scores, -1e30)
    row_peak = jnp.maximum(jnp.max(scores, axis=-1), own_score)
    raw_weights = jnp.where(live_mask, jnp.exp(scores - row_peak[..., None]), 0.0)
    own_weight = jnp.exp(own_score - row_peak)
    denominator = jnp.sum(raw_weights, axis=-1) + own_weight
    key_probs = (raw_weights / denominator[..., None]).astype(jnp.bfloat16)
    own_prob = (own_weight / denominator).astype(jnp.bfloat16)
    head_output = jnp.einsum(
        "rkgt,rtkd->rkgd", key_probs, values_part, preferred_element_type=jnp.float32
    )
    head_output = head_output + own_prob.astype(jnp.float32)[..., None] * vnew_f[:, :, None, :]
    return head_output.reshape(row_count, -1).astype(jnp.bfloat16)


def dot(a, b):
    return jnp.dot(a, b, preferred_element_type=jnp.float32)


def moe_kernel(
    att, res, gain, disp, comb, w_in, w_out, out,
    stats, xout, xbuf, big, win, wout, hid, sib_out, sib_in, far, fwd_a, fwd_b,
    step_a, step_b, sum_a, sum_b, done, home_z, pair, home_x,
    send_sem, recv_sem, local_sem,
):
    pool, grp, cuts = lax.axis_index("pool"), lax.axis_index("grp"), lax.axis_index("cuts")
    z, x = pool * 4 + grp // 4, grp % 4
    y, k = cuts // 2, cuts % 2

    def at_z(off):
        t = (z + off) % 8
        return (t // 4, (t % 4) * 4 + x, cuts)

    def at_x(off):
        return (pool, (grp // 4) * 4 + (x + off) % 4, cuts)

    def at_cut(off):
        return (pool, grp, (cuts + off) % 8)

    sibling = (pool, grp, y * 2 + (1 - k))
    up = at_cut(2)
    down = at_cut(6)

    ys = (0, 3, 1, 2)

    def cut_of(i, other):
        core = (1 - k) if other else k
        return ((y + ys[i]) % 4) * 2 + core

    weights = []
    for c in range(CUTS):
        weights.append(
            pltpu.make_async_copy(w_in.at[0, pl.ds(c * CW, CW), :], win.at[c], local_sem.at[c])
        )
    for c in range(CUTS):
        weights.append(
            pltpu.make_async_copy(
                w_out.at[0, :, pl.ds(c * CW, CW)], wout.at[c], local_sem.at[CUTS + c]
            )
        )
    for w in weights:
        w.start()

    barrier = pltpu.get_barrier_semaphore()
    peers = [at_cut(o) for o in range(1, 8)]
    peers += [at_x(o) for o in range(1, 4)]
    peers += [at_z(o) for o in range(1, 8)]
    for peer in peers:
        pl.semaphore_signal(barrier, inc=1, device_id=peer, device_id_type=MESH)

    sent = []

    def push(src, dst, where):
        i = len(sent)
        copy = pltpu.make_async_remote_copy(
            src_ref=src,
            dst_ref=dst,
            send_sem=send_sem.at[i],
            recv_sem=recv_sem.at[i],
            device_id=where,
            device_id_type=MESH,
        )
        copy.start()
        sent.append(copy)
        return copy

    stream = (res[...].astype(jnp.float32) + att[...].astype(jnp.float32)).astype(jnp.bfloat16)
    stream = stream.astype(jnp.float32)
    total = jnp.sum(stream, axis=1, keepdims=True)
    squares = jnp.sum(stream * stream, axis=1, keepdims=True)
    lane = lax.broadcasted_iota(jnp.int32, (ROWS, 128), 1)
    stats[0] = jnp.where(lane == 0, total, squares)
    pl.semaphore_wait(barrier, len(peers))
    got = [push(stats.at[0], stats.at[o], at_cut(o)) for o in range(1, 8)]
    for g in got:
        g.wait_recv()
    sums = jnp.sum(stats[...], axis=0) * (1.0 / D)
    mean = sums[:, 0:1]
    variance = sums[:, 1:2] - mean * mean
    normed = ((stream - mean) * lax.rsqrt(variance + 1e-05) * gain[...]).astype(jnp.bfloat16)

    got_x = []
    for r in (2, 1, 3, 0):
        block = dot(disp[pl.ds(r * 64, 64), :], normed).astype(jnp.bfloat16)
        if r == 0:
            for d in range(4):
                xbuf[d, 0:SLOTS, :] = block[d * SLOTS : (d + 1) * SLOTS, :]
        else:
            for d in range(4):
                xout[r - 1, d] = block[d * SLOTS : (d + 1) * SLOTS, :]
            got_x.append(
                push(xout.at[r - 1], xbuf.at[:, pl.ds(r * SLOTS, SLOTS), :], at_x(r))
            )
    for g in got_x:
        g.wait_recv()
    got_z = [None] * UNITS
    for u in range(UNITS):
        if OFFS[u] == 0:
            big[0, u] = xbuf[0]
        else:
            got_z[u] = push(xbuf.at[OFFS[u] % 4], big.at[0, u], at_z(OFFS[u]))

    a0, a1, a2 = {}, {}, {}
    b0, b1, b2, b3, b4 = {}, {}, {}, {}, {}

    def stage_a0(u):
        if got_z[u] is not None:
            got_z[u].wait_recv()
        a0[u] = (
            push(big.at[0, u], big.at[1, u], up),
            push(big.at[0, u], big.at[2, u], down),
            push(big.at[0, u], big.at[4, u], sibling),
        )

    def stage_a1(u):
        from_down, from_up, _ = a0[u]
        from_down.wait_recv()
        first = push(big.at[1, u, pl.ds(0, 32), :], big.at[3, u, pl.ds(0, 32), :], up)
        s1 = push(big.at[1, u], big.at[5, u], sibling)
        from_up.wait_recv()
        second = push(big.at[2, u, pl.ds(32, 32), :], big.at[3, u, pl.ds(32, 32), :], down)
        s2 = push(big.at[2, u], big.at[6, u], sibling)
        a1[u] = (first, second, s1, s2)

    def stage_a2(u):
        first, second, _, _ = a1[u]
        first.wait_recv()
        second.wait_recv()
        a2[u] = push(big.at[3, u], big.at[7, u], sibling)

    def stage_mm(g):
        if g == 0:
            for w in weights[:CUTS]:
                w.wait()
        for u in (2 * g, 2 * g + 1):
            a0[u][2].wait_recv()
            a1[u][2].wait_recv()
            a1[u][3].wait_recv()
            a2[u].wait_recv()
        acc = jnp.zeros((128, FF), jnp.float32)
        for s in range(8):
            rows = big[s, 2 * g : 2 * g + 2].reshape(128, CW)
            acc = acc + dot(rows, win[cut_of(s % 4, s >= 4)])
        hid[g] = (acc / (1.0 + jnp.exp(-acc))).astype(jnp.bfloat16)

    def stage_b0(g):
        if g == 0:
            for w in weights[CUTS:]:
                w.wait()
        b0[g] = {}
        for i in (3, 2, 1, 0):
            sib_out[g, i] = dot(hid[g], wout[cut_of(i, True)]).astype(jnp.bfloat16)
            b0[g][i] = push(sib_out.at[g, i], sib_in.at[g, i], sibling)

    def chip_sum(g, i):
        b0[g][i].wait_recv()
        return dot(hid[g], wout[cut_of(i, False)]) + sib_in[g, i].astype(jnp.float32)

    def stage_b1(g):
        far[g] = chip_sum(g, 3).astype(jnp.bfloat16)
        b1[g] = (
            push(far.at[g, pl.ds(0, 64), :], fwd_a.at[g], up),
            push(far.at[g, pl.ds(64, 64), :], fwd_b.at[g], down),
        )

    def stage_b2(g):
        part = chip_sum(g, 2)
        b1[g][0].wait_recv()
        sum_a[g, 0:64] = (part[0:64] + fwd_a[g].astype(jnp.float32)).astype(jnp.bfloat16)
        sum_a[g, 64:128] = part[64:128].astype(jnp.bfloat16)
        to_up = push(sum_a.at[g], step_a.at[g], up)
        part = chip_sum(g, 1)
        b1[g][1].wait_recv()
        sum_b[g, 0:64] = part[0:64].astype(jnp.bfloat16)
        sum_b[g, 64:128] = (part[64:128] + fwd_b[g].astype(jnp.float32)).astype(jnp.bfloat16)
        to_down = push(sum_b.at[g], step_b.at[g], down)
        b2[g] = (to_up, to_down)

    def stage_b3(g):
        part = chip_sum(g, 0)
        b2[g][0].wait_recv()
        b2[g][1].wait_recv()
        part = part + step_a[g].astype(jnp.float32) + step_b[g].astype(jnp.float32)
        part = part.astype(jnp.bfloat16)
        for i in range(2):
            u = 2 * g + i
            half = part[i * 64 : (i + 1) * 64]
            if OFFS[u] == 0:
                home_z[u] = half
                b3[u] = None
            else:
                done[u] = half
                b3[u] = push(done.at[u], home_z.at[u], at_z(8 - OFFS[u]))

    def stage_b4(d):
        units = [u for u in range(UNITS) if OFFS[u] % 4 == d]
        for u in units:
            if b3[u] is not None:
                b3[u].wait_recv()
        both = home_z[units[0]].astype(jnp.float32) + home_z[units[1]].astype(jnp.float32)
        both = both.astype(jnp.bfloat16)
        home_x[0, d] = both[0:SLOTS]
        pair[d] = both
        for r in (2, 1, 3):
            b4[(r, d)] = push(
                pair.at[d, pl.ds(r * SLOTS, SLOTS), :], home_x.at[r, d], at_x(4 - r)
            )

    plan = []
    for u in range(UNITS):
        plan.append((u, stage_a0, u))
        plan.append((u + 1.2, stage_a1, u))
        plan.append((u + 2.4, stage_a2, u))
    for g in range(GROUPS):
        t = 2 * g + 1
        plan.append((t + 3.6, stage_mm, g))
        plan.append((t + 3.7, stage_b0, g))
        plan.append((t + 4.8, stage_b1, g))
        plan.append((t + 6.2, stage_b2, g))
        plan.append((t + 8.1, stage_b3, g))
    for n, d in enumerate((1, 3, 2, 0)):
        plan.append((2 * n + 12, stage_b4, d))
    for _, stage, i in sorted(plan, key=lambda p: p[0]):
        stage(i)

    for copy in b4.values():
        copy.wait_recv()
    gates = comb[...]
    high = gates.astype(jnp.bfloat16)
    low = (gates - high.astype(jnp.float32)).astype(jnp.bfloat16)
    back = home_x[...].reshape(4 * 4 * SLOTS, CW)
    out[...] = (dot(high, back) + dot(low, back)).astype(jnp.bfloat16)
    for copy in sent:
        copy.wait_send()


def body(
    residual_in,
    queries,
    key_new,
    value_new,
    key_cache,
    value_cache,
    cache_lens,
    norm_gain,
    expert_ids,
    gate_weights,
    w_in,
    w_out,
):
    attended = attend_local(queries, key_new, value_new, key_cache, value_cache, cache_lens)
    grp, cuts = lax.axis_index("grp"), lax.axis_index("cuts")
    along_x = (grp % 4 + jnp.arange(4, dtype=jnp.int32)) % 4
    along_z = (grp // 4 + jnp.arange(4, dtype=jnp.int32)) % 4
    experts = (along_z[None, :] * 4 + along_x[:, None]).reshape(16)
    picks = expert_ids[:, :, None] == experts[None, None, :]
    chosen = jnp.sum(picks.astype(jnp.int32), axis=1)
    weight_table = jnp.sum(jnp.where(picks, gate_weights[:, :, None], 0.0), axis=1)
    slot_index = jnp.cumsum(chosen, axis=0) - chosen
    dispatch = (chosen[:, :, None] == 1) & (
        slot_index[:, :, None] == jnp.arange(SLOTS, dtype=jnp.int32)[None, None, :]
    )
    combine = jnp.where(dispatch, weight_table[:, :, None], 0.0).reshape(ROWS, 16 * SLOTS)
    disp = dispatch.astype(jnp.bfloat16).reshape(ROWS, 16 * SLOTS).T
    gain = lax.dynamic_slice(norm_gain, (cuts * CW,), (CW,)).reshape(1, CW)

    vmem = pl.BlockSpec(memory_space=pltpu.VMEM)
    hbm = pl.BlockSpec(memory_space=pl.ANY)
    bf = jnp.bfloat16
    expert_mix = pl.pallas_call(
        moe_kernel,
        out_shape=jax.ShapeDtypeStruct((ROWS, CW), bf),
        in_specs=[vmem] * 5 + [hbm] * 2,
        out_specs=vmem,
        scratch_shapes=[
            pltpu.VMEM((8, ROWS, 128), jnp.float32),
            pltpu.VMEM((3, 4, SLOTS, CW), bf),
            pltpu.VMEM((4, 64, CW), bf),
            pltpu.VMEM((8, UNITS, 64, CW), bf),
            pltpu.VMEM((CUTS, CW, FF), bf),
            pltpu.VMEM((CUTS, FF, CW), bf),
            pltpu.VMEM((GROUPS, 128, FF), bf),
            pltpu.VMEM((GROUPS, 4, 128, CW), bf),
            pltpu.VMEM((GROUPS, 4, 128, CW), bf),
            pltpu.VMEM((GROUPS, 128, CW), bf),
            pltpu.VMEM((GROUPS, 64, CW), bf),
            pltpu.VMEM((GROUPS, 64, CW), bf),
            pltpu.VMEM((GROUPS, 128, CW), bf),
            pltpu.VMEM((GROUPS, 128, CW), bf),
            pltpu.VMEM((GROUPS, 128, CW), bf),
            pltpu.VMEM((GROUPS, 128, CW), bf),
            pltpu.VMEM((UNITS, 64, CW), bf),
            pltpu.VMEM((UNITS, 64, CW), bf),
            pltpu.VMEM((4, 64, CW), bf),
            pltpu.VMEM((4, 4, SLOTS, CW), bf),
            pltpu.SemaphoreType.DMA((N_SEM,)),
            pltpu.SemaphoreType.DMA((N_SEM,)),
            pltpu.SemaphoreType.DMA((2 * CUTS,)),
        ],
        compiler_params=pltpu.CompilerParams(
            collective_id=0, has_side_effects=True, vmem_limit_bytes=56 * 1024 * 1024
        ),
    )(attended, residual_in, gain, disp, combine, w_in, w_out)
    return (attended, expert_mix)


def solution(mesh):
    return jax.shard_map(
        body,
        mesh=mesh,
        in_specs=(
            P(("pool", "grp"), "cuts"),
            P(("pool", "grp"), "cuts"),
            P(("pool", "grp"), "cuts"),
            P(("pool", "grp"), "cuts"),
            P(("pool", "grp"), None, "cuts"),
            P(("pool", "grp"), None, "cuts"),
            P(("pool", "grp")),
            P(),
            P(("pool", "grp"), None),
            P(("pool", "grp"), None),
            P("grp", None, ("pool", "cuts")),
            P("grp", ("pool", "cuts"), None),
        ),
        out_specs=(P(("pool", "grp"), "cuts"), P(("pool", "grp"), "cuts")),
        check_vma=False,
    )
```

```python
import math

import jax
import jax.numpy as jnp
from jax import lax
from jax.experimental import pallas as pl
from jax.experimental.pallas import tpu as pltpu
from jax.sharding import PartitionSpec as P

MESH = pl.DeviceIdType.MESH
BF, F32 = jnp.bfloat16, jnp.float32
OFFS = (0, 1, 7, 2, 6, 3, 5, 4)
UNITS = 8
UR = 64
ALL = UNITS * UR
SLOTS = 16
CW = 768
CUTS = 8
FF = 384
D = CUTS * CW
ROWS = 32
HEADS = 6
SPAN = 128
HD = 128
N_SEM = 160
FWD = ((0, 1), (2, 3), (4, 5), (6, 7))
BWD = ((2, 3), (4, 5), (6, 7), (1,), (0,))


def dot(a, b):
    return jnp.dot(a, b, preferred_element_type=F32)


def attention(q, knew, vnew, lens, kbuf, vbuf, kv_loads, q3, s3, o3):
    scale = 1.0 / math.sqrt(HD)
    q3[...] = jnp.zeros(q3.shape, F32)
    for h in range(HEADS):
        q3[:, h, :] = q[:, h * HD : (h + 1) * HD].astype(F32)
    new_k, new_v = knew[...].astype(F32), vnew[...].astype(F32)
    lane = lax.broadcasted_iota(jnp.int32, (8, SPAN), 1)
    for w in kv_loads[: len(kv_loads) // 2]:
        w.wait()
    own = []
    for r in range(ROWS):
        qr = q3[r]
        s = lax.dot_general(
            qr.astype(BF), kbuf[r], (((1,), (1,)), ((), ())), preferred_element_type=F32
        )
        s3[r] = jnp.where(lane < lens[r], s * scale, -1e30)
        own.append(jnp.sum(qr * new_k[r : r + 1, :], axis=1, keepdims=True) * scale)
    for w in kv_loads[len(kv_loads) // 2 :]:
        w.wait()
    for r in range(ROWS):
        s = s3[r]
        peak = jnp.maximum(jnp.max(s, axis=1, keepdims=True), own[r])
        raw = jnp.where(lane < lens[r], jnp.exp(s - peak), 0.0)
        own_raw = jnp.exp(own[r] - peak)
        total = jnp.sum(raw, axis=1, keepdims=True) + own_raw
        probs = (raw / total).astype(BF)
        own_prob = (own_raw / total).astype(BF).astype(F32)
        o3[r] = dot(probs, vbuf[r]) + own_prob * new_v[r : r + 1, :]


def routing(ids, gates, x, zl):
    j = lax.broadcasted_iota(jnp.int32, (16, ROWS), 0)
    expert = (((zl + (j & 3)) & 3) << 2) + ((x + (j >> 2)) & 3)
    chosen = jnp.zeros((16, ROWS), F32)
    weight = jnp.zeros((16, ROWS), F32)
    for t in range(4):
        hit = ids[t : t + 1, :] == expert
        chosen = chosen + jnp.where(hit, 1.0, 0.0)
        weight = weight + jnp.where(hit, gates[t : t + 1, :], 0.0)
    before = lax.broadcasted_iota(jnp.int32, (ROWS, ROWS), 0) < lax.broadcasted_iota(
        jnp.int32, (ROWS, ROWS), 1
    )
    slot = dot(chosen.astype(BF), jnp.where(before, 1.0, 0.0).astype(BF))
    spread = (lax.broadcasted_iota(jnp.int32, (256, 16), 0) >> 4) == (
        lax.broadcasted_iota(jnp.int32, (256, 16), 1)
    )
    spread = jnp.where(spread, 1.0, 0.0).astype(BF)
    high = weight.astype(BF)
    low = (weight - high.astype(F32)).astype(BF)
    place = (lax.broadcasted_iota(jnp.int32, (256, ROWS), 0) & 15).astype(F32)
    here = (dot(spread, chosen.astype(BF)) > 0.5) & (dot(spread, slot.astype(BF)) == place)
    disp = jnp.where(here, 1.0, 0.0).astype(BF)
    high = jnp.where(here, dot(spread, high), 0.0).T.astype(BF)
    low = jnp.where(here, dot(spread, low), 0.0).T.astype(BF)
    return disp, high, low


def moe_kernel(
    q, res, knew, vnew, kc, vc, lens, gain, ids, gates, w_in, w_out, out, att_out,
    kbuf, vbuf, q3, s3, o3, xout, xbuf, big, win, wout, acc, hid, sib_out, sib_in, far, fwd,
    step_a, step_b, sum_a, sum_b, done, home_z, pair, home_x,
    send_sem, recv_sem, local_sem,
):
    pool, grp, cuts = lax.axis_index("pool"), lax.axis_index("grp"), lax.axis_index("cuts")
    zl, x = grp // 4, grp % 4
    z = pool * 4 + zl
    y, k = cuts // 2, cuts % 2

    def at_z(off):
        t = (z + off) % 8
        return (t // 4, (t % 4) * 4 + x, cuts)

    def at_x(off):
        return (pool, zl * 4 + (x + off) % 4, cuts)

    sibling = (pool, grp, y * 2 + (1 - k))
    up = (pool, grp, (cuts + 2) % 8)
    down = (pool, grp, (cuts + 6) % 8)

    ys = (0, 3, 1, 2)

    def cut_of(s):
        core = k if s < 4 else 1 - k
        return ((y + ys[s % 4]) % 4) * 2 + core

    def load(src, dst, i):
        copy = pltpu.make_async_copy(src, dst, local_sem.at[i])
        copy.start()
        return copy

    kv_loads = [load(kc, kbuf, 0), load(vc, vbuf, 1)]

    barrier = pltpu.get_barrier_semaphore()
    peers = [sibling, up, down]
    peers += [at_x(o) for o in range(1, 4)]
    peers += [at_z(o) for o in range(1, 8)]
    for peer in peers:
        pl.semaphore_signal(barrier, inc=1, device_id=peer, device_id_type=MESH)

    sent, left = [], []

    def wait_left(copies):
        for copy in copies:
            copy.wait_send()
            left.append(copy)

    def push(src, dst, where):
        i = len(sent)
        copy = pltpu.make_async_remote_copy(
            src_ref=src,
            dst_ref=dst,
            send_sem=send_sem.at[i],
            recv_sem=recv_sem.at[i],
            device_id=where,
            device_id_type=MESH,
        )
        copy.start()
        sent.append(copy)
        return copy

    disp, high, low = routing(ids, gates, x, zl)
    attention(q, knew, vnew, lens, kbuf, vbuf, kv_loads, q3, s3, o3)
    in_loads = [
        load(
            w_in.at[0, pl.ds(pl.multiple_of(cut_of(s) * CW, CW), CW), :], win.at[s], 2 + s
        )
        for s in range(CUTS)
    ]
    out_loads = [
        load(
            w_out.at[0, :, pl.ds(pl.multiple_of(cut_of(s) * CW, CW), CW)], wout.at[s], 10 + s
        )
        for s in range(CUTS)
    ]
    for h in range(HEADS):
        att_out[:, h * HD : (h + 1) * HD] = o3[:, h, :].astype(BF).astype(F32)
    stream = (res[...].astype(F32) + att_out[...]).astype(BF)

    blocks = dot(disp, stream).astype(BF)
    got_x = {}
    pl.semaphore_wait(barrier, len(peers))

    def start_x(d):
        for r in range(4):
            block = blocks[(r * 4 + d) * SLOTS : (r * 4 + d + 1) * SLOTS]
            if r == 0:
                xbuf[d, 0:SLOTS, :] = block
            else:
                xout[d, r] = block
        for r in (2, 1, 3):
            got_x[d, r] = push(xout.at[d, r], xbuf.at[d, pl.ds(r * SLOTS, SLOTS), :], at_x(r))

    start_x(0)
    wait_left([got_x[0, r] for r in (1, 2, 3)])
    start_x(1)
    start_x(3)

    a0, a1, a2, got_z = {}, {}, {}, {}
    b0, b1, b2, b3, b4 = {}, {}, {}, {}, {}

    def rows_of(units):
        return units[0] * UR, len(units) * UR

    def stage_x(d):
        for r in (2, 1, 3):
            got_x[d, r].wait_recv()
        if d == 0:
            big[0, 0:UR] = xbuf[0]
        if d == 1:
            start_x(2)

    def stage_z(u):
        got_z[u] = push(xbuf.at[OFFS[u] % 4], big.at[0, pl.ds(u * UR, UR)], at_z(OFFS[u]))

    def stage_a0(u):
        if OFFS[u] != 0:
            got_z[u].wait_recv()
        at = pl.ds(u * UR, UR)
        a0[u] = (
            push(big.at[0, at], big.at[1, at], up),
            push(big.at[0, at], big.at[2, at], down),
            push(big.at[0, at], big.at[4, at], sibling),
        )

    def stage_a1(u):
        at, top, bottom = pl.ds(u * UR, UR), pl.ds(u * UR, 32), pl.ds(u * UR + 32, 32)
        from_down, from_up, _ = a0[u]
        from_down.wait_recv()
        first = push(big.at[1, top], big.at[3, top], up)
        s1 = push(big.at[1, at], big.at[5, at], sibling)
        from_up.wait_recv()
        second = push(big.at[2, bottom], big.at[3, bottom], down)
        s2 = push(big.at[2, at], big.at[6, at], sibling)
        a1[u] = (first, second, s1, s2)

    def stage_a2(u):
        first, second, _, _ = a1[u]
        first.wait_recv()
        second.wait_recv()
        at = pl.ds(u * UR, UR)
        a2[u] = push(big.at[3, at], big.at[7, at], sibling)

    def stage_mm(units):
        if units == FWD[0]:
            for w in in_loads:
                w.wait()
        for u in units:
            a0[u][2].wait_recv()
            a1[u][2].wait_recv()
            a1[u][3].wait_recv()
            a2[u].wait_recv()
        base, n = rows_of(units)
        at = slice(base, base + n)

        def add_stats(s, sums):
            total, squares = sums
            rows = big[s, at, :].astype(F32)
            for l in range(CW // 128):
                v = rows[:, l * 128 : (l + 1) * 128]
                total = total + v
                squares = squares + v * v
            return total, squares

        zero = jnp.zeros((n, 128), F32)
        total, squares = lax.fori_loop(0, CUTS, add_stats, (zero, zero))
        mean = jnp.sum(total, axis=1, keepdims=True) * (1.0 / D)
        variance = jnp.sum(squares, axis=1, keepdims=True) * (1.0 / D) - mean * mean
        scale = lax.rsqrt(variance + 1e-05)
        for s in range(CUTS):
            rows = big[s, at, :].astype(F32)
            factor = gain[:, pl.ds(pl.multiple_of(cut_of(s) * CW, CW), CW)]
            normed = ((rows - mean) * scale * factor).astype(BF)
            part = dot(normed, win[s])
            if s == 0:
                acc[0:n] = part
            elif s < CUTS - 1:
                acc[0:n] += part
        inner = acc[0:n] + part
        hid[at, :] = (inner / (1.0 + jnp.exp(-inner))).astype(BF)

    def stage_b0(units):
        if units == (1,):
            for w in out_loads:
                w.wait()
        base, n = rows_of(units)
        at = pl.ds(base, n)
        mine = hid[base : base + n]
        b0[units] = {}
        for i in (3, 2, 1, 0):
            sib_out[i, at] = dot(mine, wout[4 + i]).astype(BF)
            b0[units][i] = push(sib_out.at[i, at], sib_in.at[i, at], sibling)

    def chip_sum(units, i):
        base, n = rows_of(units)
        part = dot(hid[base : base + n], wout[i])
        b0[units][i].wait_recv()
        return part + sib_in[i, base : base + n].astype(F32)

    def stage_b1(units):
        base, n = rows_of(units)
        h = n // 2
        far[base : base + n] = chip_sum(units, 3).astype(BF)
        top, bottom = pl.ds(base, h), pl.ds(base + h, h)
        b1[units] = (
            push(far.at[top], fwd.at[top], up),
            push(far.at[bottom], fwd.at[bottom], down),
        )

    def stage_b2(units):
        base, n = rows_of(units)
        h, at = n // 2, pl.ds(base, n)
        part = chip_sum(units, 2)
        b1[units][0].wait_recv()
        sum_a[base : base + h] = (part[0:h] + fwd[base : base + h].astype(F32)).astype(BF)
        sum_a[base + h : base + n] = part[h:n].astype(BF)
        to_up = push(sum_a.at[at], step_a.at[at], up)
        part = chip_sum(units, 1)
        b1[units][1].wait_recv()
        sum_b[base : base + h] = part[0:h].astype(BF)
        sum_b[base + h : base + n] = (
            part[h:n] + fwd[base + h : base + n].astype(F32)
        ).astype(BF)
        to_down = push(sum_b.at[at], step_b.at[at], down)
        b2[units] = (to_up, to_down)

    def stage_b3(units):
        base, n = rows_of(units)
        part = chip_sum(units, 0)
        b2[units][0].wait_recv()
        b2[units][1].wait_recv()
        part = part + step_a[base : base + n].astype(F32) + step_b[base : base + n].astype(F32)
        part = part.astype(BF)
        for i, u in enumerate(units):
            half = part[i * UR : (i + 1) * UR]
            if OFFS[u] == 0:
                home_z[u] = half
            else:
                done[u] = half
                b3[u] = push(done.at[u], home_z.at[u], at_z(8 - OFFS[u]))

    def stage_b4(d):
        units = [u for u in range(UNITS) if OFFS[u] % 4 == d]
        for u in units:
            if OFFS[u] != 0:
                b3[u].wait_recv()
        both = home_z[units[0]].astype(F32) + home_z[units[1]].astype(F32)
        both = both.astype(BF)
        home_x[0, d] = both[0:SLOTS]
        pair[d] = both
        for r in (2, 1, 3):
            b4[r, d] = push(
                pair.at[d, pl.ds(r * SLOTS, SLOTS), :], home_x.at[r, d], at_x(4 - r)
            )

    plan = []
    for d, t in ((0, -1), (1, 0.1), (3, 0.2), (2, 0.3)):
        plan.append((t, stage_x, d))
    for u, t in ((1, 0.11), (2, 0.21), (3, 0.31), (4, 0.32), (5, 2.05), (6, 2.06), (7, 4.05)):
        plan.append((t, stage_z, u))
    for u in range(UNITS):
        plan.append((u, stage_a0, u))
        plan.append((u + 1.2, stage_a1, u))
        plan.append((u + 2.4, stage_a2, u))
    for units in FWD:
        plan.append((units[-1] + 3.6, stage_mm, units))
    for units, t0, t1, t2, t3 in (
        ((2, 3), 6.7, 7.8, 9.21, 11.1),
        ((4, 5), 8.7, 9.8, 11.21, 13.1),
        ((6, 7), 10.7, 11.8, 13.21, 15.1),
        ((1,), 4.7, 10.0, 13.41, 15.3),
        ((0,), 4.75, 10.1, 13.61, 15.5),
    ):
        plan.append((t0, stage_b0, units))
        plan.append((t1, stage_b1, units))
        plan.append((t2, stage_b2, units))
        plan.append((t3, stage_b3, units))
    for d, t in ((3, 15.04), (2, 15.05), (1, 16), (0, 16.1)):
        plan.append((t, stage_b4, d))
    for _, stage, i in sorted(plan, key=lambda p: p[0]):
        stage(i)

    for copy in b4.values():
        copy.wait_recv()
    back = home_x[...].reshape(4 * 4 * SLOTS, CW)
    out[...] = dot(high, back) + dot(low, back)
    for copy in sent:
        if all(copy is not c for c in left):
            copy.wait_send()


def body(
    residual_in,
    queries,
    key_new,
    value_new,
    key_cache,
    value_cache,
    cache_lens,
    norm_gain,
    expert_ids,
    gate_weights,
    w_in,
    w_out,
):
    vmem = pl.BlockSpec(memory_space=pltpu.VMEM)
    smem = pl.BlockSpec(memory_space=pltpu.SMEM)
    hbm = pl.BlockSpec(memory_space=pl.ANY)
    expert_mix, attended = pl.pallas_call(
        moe_kernel,
        out_shape=(
            jax.ShapeDtypeStruct((ROWS, CW), F32),
            jax.ShapeDtypeStruct((ROWS, CW), F32),
        ),
        in_specs=[vmem] * 4 + [hbm] * 2 + [smem] + [vmem] * 3 + [hbm] * 2,
        out_specs=(vmem, vmem),
        scratch_shapes=[
            pltpu.VMEM((ROWS, SPAN, HD), BF),
            pltpu.VMEM((ROWS, SPAN, HD), BF),
            pltpu.VMEM((ROWS, 8, HD), F32),
            pltpu.VMEM((ROWS, 8, SPAN), F32),
            pltpu.VMEM((ROWS, 8, HD), F32),
            pltpu.VMEM((4, 4, SLOTS, CW), BF),
            pltpu.VMEM((4, UR, CW), BF),
            pltpu.VMEM((CUTS, ALL, CW), BF),
            pltpu.VMEM((CUTS, CW, FF), BF),
            pltpu.VMEM((CUTS, FF, CW), BF),
            pltpu.VMEM((2 * UR, FF), F32),
            pltpu.VMEM((ALL, FF), BF),
            pltpu.VMEM((4, ALL, CW), BF),
            pltpu.VMEM((4, ALL, CW), BF),
            pltpu.VMEM((ALL, CW), BF),
            pltpu.VMEM((ALL, CW), BF),
            pltpu.VMEM((ALL, CW), BF),
            pltpu.VMEM((ALL, CW), BF),
            pltpu.VMEM((ALL, CW), BF),
            pltpu.VMEM((ALL, CW), BF),
            pltpu.VMEM((UNITS, UR, CW), BF),
            pltpu.VMEM((UNITS, UR, CW), BF),
            pltpu.VMEM((4, UR, CW), BF),
            pltpu.VMEM((4, 4, SLOTS, CW), BF),
            pltpu.SemaphoreType.DMA((N_SEM,)),
            pltpu.SemaphoreType.DMA((N_SEM,)),
            pltpu.SemaphoreType.DMA((2 + 2 * CUTS,)),
        ],
        compiler_params=pltpu.CompilerParams(
            collective_id=0, has_side_effects=True, vmem_limit_bytes=56 * 1024 * 1024
        ),
    )(
        queries,
        residual_in,
        key_new,
        value_new,
        key_cache,
        value_cache,
        cache_lens,
        norm_gain.reshape(1, D),
        expert_ids.T,
        gate_weights.T,
        w_in,
        w_out,
    )
    return (attended.astype(BF), expert_mix.astype(BF))


def solution(mesh):
    return jax.shard_map(
        body,
        mesh=mesh,
        in_specs=(
            P(("pool", "grp"), "cuts"),
            P(("pool", "grp"), "cuts"),
            P(("pool", "grp"), "cuts"),
            P(("pool", "grp"), "cuts"),
            P(("pool", "grp"), None, "cuts"),
            P(("pool", "grp"), None, "cuts"),
            P(("pool", "grp")),
            P(),
            P(("pool", "grp"), None),
            P(("pool", "grp"), None),
            P("grp", None, ("pool", "cuts")),
            P("grp", ("pool", "cuts"), None),
        ),
        out_specs=(P(("pool", "grp"), "cuts"), P(("pool", "grp"), "cuts")),
        check_vma=False,
    )
```

```python
import math

import jax
import jax.numpy as jnp
from jax import lax
from jax.experimental import pallas as pl
from jax.experimental.pallas import tpu as pltpu
from jax.sharding import PartitionSpec as P

MESH = pl.DeviceIdType.MESH
BF, F32 = jnp.bfloat16, jnp.float32
OFFS = (0, 1, 7, 2, 6, 3, 5, 4)
UNITS = 8
UR = 64
ALL = UNITS * UR
SLOTS = 16
CW = 768
CUTS = 8
FF = 384
D = CUTS * CW
ROWS = 32
HEADS = 6
SPAN = 128
HD = 128
N_SEM = 160
PLAN = (
    ("sx", 3), ("sx", 0), ("sx", 2), ("sx", 1), ("x", 3), ("z", 2), ("z", 5), ("x", 0), ("a0", 0),
    ("x", 2), ("z", 4), ("z", 3), ("x", 1), ("z", 1), ("a0", 2), ("a1", 0), ("a1", 2), ("a0", 4),
    ("z", 7), ("a0", 5), ("a1", 4), ("z", 6), ("a0", 3), ("a2", 4), ("a1", 5), ("a0", 1),
    ("a2", 5), ("a1", 3), ("a0", 7), ("mm", (4, 5)), ("a2", 3), ("a0", 6), ("a2", 2), ("a1", 7),
    ("a2", 0), ("b0", (4, 5)), ("b1", (4, 5)), ("mm", (2, 3)), ("a1", 6), ("a2", 7), ("a1", 1),
    ("b0", (2, 3)), ("b2", (4, 5)), ("a2", 6), ("mm", (6, 7)), ("b1", (2, 3)), ("a2", 1),
    ("b0", (6, 7)), ("b1", (6, 7)), ("mm", (0, 1)), ("b2", (2, 3)), ("b3", (4, 5)),
    ("b2", (6, 7)), ("b0", (0, 1)), ("b1", (0, 1)), ("b3", (2, 3)), ("b4", 3), ("b3", (6, 7)),
    ("b2", (0, 1)), ("b4", 2), ("b3", (0, 1)), ("b4", 1), ("b4", 0),
)
FIRST_MM = (4, 5)
FIRST_B0 = (4, 5)


def dot(a, b):
    return jnp.dot(a, b, preferred_element_type=F32)


def attention(q, knew, vnew, lens, kbuf, vbuf, kv_loads, q3, s3, o3):
    scale = 1.0 / math.sqrt(HD)
    q3[...] = jnp.zeros(q3.shape, F32)
    for h in range(HEADS):
        q3[:, h, :] = q[:, h * HD : (h + 1) * HD].astype(F32)
    new_k, new_v = knew[...].astype(F32), vnew[...].astype(F32)
    lane = lax.broadcasted_iota(jnp.int32, (8, SPAN), 1)
    for w in kv_loads[: len(kv_loads) // 2]:
        w.wait()
    own = []
    for r in range(ROWS):
        qr = q3[r]
        s = lax.dot_general(
            qr.astype(BF), kbuf[r], (((1,), (1,)), ((), ())), preferred_element_type=F32
        )
        s3[r] = jnp.where(lane < lens[r], s * scale, -1e30)
        own.append(jnp.sum(qr * new_k[r : r + 1, :], axis=1, keepdims=True) * scale)
    for w in kv_loads[len(kv_loads) // 2 :]:
        w.wait()
    for r in range(ROWS):
        s = s3[r]
        peak = jnp.maximum(jnp.max(s, axis=1, keepdims=True), own[r])
        raw = jnp.where(lane < lens[r], jnp.exp(s - peak), 0.0)
        own_raw = jnp.exp(own[r] - peak)
        total = jnp.sum(raw, axis=1, keepdims=True) + own_raw
        probs = (raw / total).astype(BF)
        own_prob = (own_raw / total).astype(BF).astype(F32)
        o3[r] = dot(probs, vbuf[r]) + own_prob * new_v[r : r + 1, :]


def routing(ids, gates, x, zl):
    j = lax.broadcasted_iota(jnp.int32, (16, ROWS), 0)
    expert = (((zl + (j & 3)) & 3) << 2) + ((x + (j >> 2)) & 3)
    chosen = jnp.zeros((16, ROWS), F32)
    weight = jnp.zeros((16, ROWS), F32)
    for t in range(4):
        hit = ids[t : t + 1, :] == expert
        chosen = chosen + jnp.where(hit, 1.0, 0.0)
        weight = weight + jnp.where(hit, gates[t : t + 1, :], 0.0)
    before = lax.broadcasted_iota(jnp.int32, (ROWS, ROWS), 0) < lax.broadcasted_iota(
        jnp.int32, (ROWS, ROWS), 1
    )
    slot = dot(chosen.astype(BF), jnp.where(before, 1.0, 0.0).astype(BF))
    spread = (lax.broadcasted_iota(jnp.int32, (256, 16), 0) >> 4) == (
        lax.broadcasted_iota(jnp.int32, (256, 16), 1)
    )
    spread = jnp.where(spread, 1.0, 0.0).astype(BF)
    high = weight.astype(BF)
    low = (weight - high.astype(F32)).astype(BF)
    place = (lax.broadcasted_iota(jnp.int32, (256, ROWS), 0) & 15).astype(F32)
    here = (dot(spread, chosen.astype(BF)) > 0.5) & (dot(spread, slot.astype(BF)) == place)
    disp = jnp.where(here, 1.0, 0.0).astype(BF)
    high = jnp.where(here, dot(spread, high), 0.0).T.astype(BF)
    low = jnp.where(here, dot(spread, low), 0.0).T.astype(BF)
    return disp, high, low


def moe_kernel(
    q, res, knew, vnew, kc, vc, lens, gain, ids, gates, w_in, w_out, out, att_out,
    kbuf, vbuf, q3, s3, o3, xout, xbuf, big, win, wout, acc, hid, sib_out, sib_in, far, fwd,
    step_a, step_b, sum_a, sum_b, done, home_z, pair, home_x,
    send_sem, recv_sem, local_sem,
):
    pool, grp, cuts = lax.axis_index("pool"), lax.axis_index("grp"), lax.axis_index("cuts")
    zl, x = grp // 4, grp % 4
    z = pool * 4 + zl
    y, k = cuts // 2, cuts % 2

    def at_z(off):
        t = (z + off) % 8
        return (t // 4, (t % 4) * 4 + x, cuts)

    def at_x(off):
        return (pool, zl * 4 + (x + off) % 4, cuts)

    sibling = (pool, grp, y * 2 + (1 - k))
    up = (pool, grp, (cuts + 2) % 8)
    down = (pool, grp, (cuts + 6) % 8)

    ys = (0, 3, 1, 2)

    def cut_of(s):
        core = k if s < 4 else 1 - k
        return ((y + ys[s % 4]) % 4) * 2 + core

    def load(src, dst, i):
        copy = pltpu.make_async_copy(src, dst, local_sem.at[i])
        copy.start()
        return copy

    kv_loads = [load(kc, kbuf, 0), load(vc, vbuf, 1)]

    barrier = pltpu.get_barrier_semaphore()
    peers = [sibling, up, down]
    peers += [at_x(o) for o in range(1, 4)]
    peers += [at_z(o) for o in range(1, 8)]
    for peer in peers:
        pl.semaphore_signal(barrier, inc=1, device_id=peer, device_id_type=MESH)

    sent = []

    def push(src, dst, where):
        i = len(sent)
        copy = pltpu.make_async_remote_copy(
            src_ref=src,
            dst_ref=dst,
            send_sem=send_sem.at[i],
            recv_sem=recv_sem.at[i],
            device_id=where,
            device_id_type=MESH,
        )
        copy.start()
        sent.append(copy)
        return copy

    disp, high, low = routing(ids, gates, x, zl)
    attention(q, knew, vnew, lens, kbuf, vbuf, kv_loads, q3, s3, o3)
    in_loads = [
        load(
            w_in.at[0, pl.ds(pl.multiple_of(cut_of(s) * CW, CW), CW), :], win.at[s], 2 + s
        )
        for s in range(CUTS)
    ]
    out_loads = [
        load(
            w_out.at[0, :, pl.ds(pl.multiple_of(cut_of(s) * CW, CW), CW)], wout.at[s], 10 + s
        )
        for s in range(CUTS)
    ]
    for h in range(HEADS):
        att_out[:, h * HD : (h + 1) * HD] = o3[:, h, :].astype(BF).astype(F32)
    stream = (res[...].astype(F32) + att_out[...]).astype(BF)

    blocks = dot(disp, stream).astype(BF)
    got_x = {}
    pl.semaphore_wait(barrier, len(peers))

    def start_x(d):
        for r in range(4):
            block = blocks[(r * 4 + d) * SLOTS : (r * 4 + d + 1) * SLOTS]
            if r == 0:
                xbuf[d, 0:SLOTS, :] = block
            else:
                xout[d, r] = block
        for r in (2, 1, 3):
            got_x[d, r] = push(xout.at[d, r], xbuf.at[d, pl.ds(r * SLOTS, SLOTS), :], at_x(r))

    a0, a1, a2, got_z = {}, {}, {}, {}
    b0, b1, b2, b3, b4 = {}, {}, {}, {}, {}

    def rows_of(units):
        return units[0] * UR, len(units) * UR

    def stage_x(d):
        for r in (2, 1, 3):
            got_x[d, r].wait_recv()
        if d == 0:
            big[0, 0:UR] = xbuf[0]

    def stage_z(u):
        got_z[u] = push(xbuf.at[OFFS[u] % 4], big.at[0, pl.ds(u * UR, UR)], at_z(OFFS[u]))

    def stage_a0(u):
        if OFFS[u] != 0:
            got_z[u].wait_recv()
        at = pl.ds(u * UR, UR)
        a0[u] = (
            push(big.at[0, at], big.at[1, at], up),
            push(big.at[0, at], big.at[2, at], down),
            push(big.at[0, at], big.at[4, at], sibling),
        )

    def stage_a1(u):
        at, top, bottom = pl.ds(u * UR, UR), pl.ds(u * UR, 32), pl.ds(u * UR + 32, 32)
        from_down, from_up, _ = a0[u]
        from_down.wait_recv()
        first = push(big.at[1, top], big.at[3, top], up)
        s1 = push(big.at[1, at], big.at[5, at], sibling)
        from_up.wait_recv()
        second = push(big.at[2, bottom], big.at[3, bottom], down)
        s2 = push(big.at[2, at], big.at[6, at], sibling)
        a1[u] = (first, second, s1, s2)

    def stage_a2(u):
        first, second, _, _ = a1[u]
        first.wait_recv()
        second.wait_recv()
        at = pl.ds(u * UR, UR)
        a2[u] = push(big.at[3, at], big.at[7, at], sibling)

    def stage_mm(units):
        if units == FIRST_MM:
            for w in in_loads:
                w.wait()
        for u in units:
            a0[u][2].wait_recv()
            a1[u][2].wait_recv()
            a1[u][3].wait_recv()
            a2[u].wait_recv()
        base, n = rows_of(units)
        at = slice(base, base + n)

        def add_stats(s, sums):
            total, squares = sums
            rows = big[s, at, :].astype(F32)
            for l in range(CW // 128):
                v = rows[:, l * 128 : (l + 1) * 128]
                total = total + v
                squares = squares + v * v
            return total, squares

        zero = jnp.zeros((n, 128), F32)
        total, squares = lax.fori_loop(0, CUTS, add_stats, (zero, zero))
        mean = jnp.sum(total, axis=1, keepdims=True) * (1.0 / D)
        variance = jnp.sum(squares, axis=1, keepdims=True) * (1.0 / D) - mean * mean
        scale = lax.rsqrt(variance + 1e-05)
        for s in range(CUTS):
            rows = big[s, at, :].astype(F32)
            factor = gain[:, pl.ds(pl.multiple_of(cut_of(s) * CW, CW), CW)]
            normed = ((rows - mean) * scale * factor).astype(BF)
            part = dot(normed, win[s])
            if s == 0:
                acc[0:n] = part
            elif s < CUTS - 1:
                acc[0:n] += part
        inner = acc[0:n] + part
        hid[at, :] = (inner / (1.0 + jnp.exp(-inner))).astype(BF)

    def stage_b0(units):
        if units == FIRST_B0:
            for w in out_loads:
                w.wait()
        base, n = rows_of(units)
        at = pl.ds(base, n)
        mine = hid[base : base + n]
        b0[units] = {}
        for i in (3, 2, 1, 0):
            sib_out[i, at] = dot(mine, wout[4 + i]).astype(BF)
            b0[units][i] = push(sib_out.at[i, at], sib_in.at[i, at], sibling)

    def chip_sum(units, i):
        base, n = rows_of(units)
        part = dot(hid[base : base + n], wout[i])
        b0[units][i].wait_recv()
        return part + sib_in[i, base : base + n].astype(F32)

    def stage_b1(units):
        base, n = rows_of(units)
        h = n // 2
        far[base : base + n] = chip_sum(units, 3).astype(BF)
        top, bottom = pl.ds(base, h), pl.ds(base + h, h)
        b1[units] = (
            push(far.at[top], fwd.at[top], up),
            push(far.at[bottom], fwd.at[bottom], down),
        )

    def stage_b2(units):
        base, n = rows_of(units)
        h, at = n // 2, pl.ds(base, n)
        part = chip_sum(units, 2)
        b1[units][0].wait_recv()
        sum_a[base : base + h] = (part[0:h] + fwd[base : base + h].astype(F32)).astype(BF)
        sum_a[base + h : base + n] = part[h:n].astype(BF)
        to_up = push(sum_a.at[at], step_a.at[at], up)
        part = chip_sum(units, 1)
        b1[units][1].wait_recv()
        sum_b[base : base + h] = part[0:h].astype(BF)
        sum_b[base + h : base + n] = (
            part[h:n] + fwd[base + h : base + n].astype(F32)
        ).astype(BF)
        to_down = push(sum_b.at[at], step_b.at[at], down)
        b2[units] = (to_up, to_down)

    def stage_b3(units):
        base, n = rows_of(units)
        part = chip_sum(units, 0)
        b2[units][0].wait_recv()
        b2[units][1].wait_recv()
        part = part + step_a[base : base + n].astype(F32) + step_b[base : base + n].astype(F32)
        part = part.astype(BF)
        for i, u in enumerate(units):
            half = part[i * UR : (i + 1) * UR]
            if OFFS[u] == 0:
                home_z[u] = half
            else:
                done[u] = half
                b3[u] = push(done.at[u], home_z.at[u], at_z(8 - OFFS[u]))

    def stage_b4(d):
        units = [u for u in range(UNITS) if OFFS[u] % 4 == d]
        for u in units:
            if OFFS[u] != 0:
                b3[u].wait_recv()
        both = home_z[units[0]].astype(F32) + home_z[units[1]].astype(F32)
        both = both.astype(BF)
        home_x[0, d] = both[0:SLOTS]
        pair[d] = both
        for r in (2, 1, 3):
            b4[r, d] = push(
                pair.at[d, pl.ds(r * SLOTS, SLOTS), :], home_x.at[r, d], at_x(4 - r)
            )

    stages = {
        "sx": start_x, "x": stage_x, "z": stage_z, "a0": stage_a0, "a1": stage_a1, "a2": stage_a2,
        "mm": stage_mm, "b0": stage_b0, "b1": stage_b1, "b2": stage_b2, "b3": stage_b3,
        "b4": stage_b4,
    }
    for name, i in PLAN:
        stages[name](i)

    for copy in b4.values():
        copy.wait_recv()
    back = home_x[...].reshape(4 * 4 * SLOTS, CW)
    out[...] = dot(high, back) + dot(low, back)
    for copy in sent:
        copy.wait_send()


def body(
    residual_in,
    queries,
    key_new,
    value_new,
    key_cache,
    value_cache,
    cache_lens,
    norm_gain,
    expert_ids,
    gate_weights,
    w_in,
    w_out,
):
    vmem = pl.BlockSpec(memory_space=pltpu.VMEM)
    smem = pl.BlockSpec(memory_space=pltpu.SMEM)
    hbm = pl.BlockSpec(memory_space=pl.ANY)
    expert_mix, attended = pl.pallas_call(
        moe_kernel,
        out_shape=(
            jax.ShapeDtypeStruct((ROWS, CW), F32),
            jax.ShapeDtypeStruct((ROWS, CW), F32),
        ),
        in_specs=[vmem] * 4 + [hbm] * 2 + [smem] + [vmem] * 3 + [hbm] * 2,
        out_specs=(vmem, vmem),
        scratch_shapes=[
            pltpu.VMEM((ROWS, SPAN, HD), BF),
            pltpu.VMEM((ROWS, SPAN, HD), BF),
            pltpu.VMEM((ROWS, 8, HD), F32),
            pltpu.VMEM((ROWS, 8, SPAN), F32),
            pltpu.VMEM((ROWS, 8, HD), F32),
            pltpu.VMEM((4, 4, SLOTS, CW), BF),
            pltpu.VMEM((4, UR, CW), BF),
            pltpu.VMEM((CUTS, ALL, CW), BF),
            pltpu.VMEM((CUTS, CW, FF), BF),
            pltpu.VMEM((CUTS, FF, CW), BF),
            pltpu.VMEM((2 * UR, FF), F32),
            pltpu.VMEM((ALL, FF), BF),
            pltpu.VMEM((4, ALL, CW), BF),
            pltpu.VMEM((4, ALL, CW), BF),
            pltpu.VMEM((ALL, CW), BF),
            pltpu.VMEM((ALL, CW), BF),
            pltpu.VMEM((ALL, CW), BF),
            pltpu.VMEM((ALL, CW), BF),
            pltpu.VMEM((ALL, CW), BF),
            pltpu.VMEM((ALL, CW), BF),
            pltpu.VMEM((UNITS, UR, CW), BF),
            pltpu.VMEM((UNITS, UR, CW), BF),
            pltpu.VMEM((4, UR, CW), BF),
            pltpu.VMEM((4, 4, SLOTS, CW), BF),
            pltpu.SemaphoreType.DMA((N_SEM,)),
            pltpu.SemaphoreType.DMA((N_SEM,)),
            pltpu.SemaphoreType.DMA((2 + 2 * CUTS,)),
        ],
        compiler_params=pltpu.CompilerParams(
            collective_id=0, has_side_effects=True, vmem_limit_bytes=56 * 1024 * 1024
        ),
    )(
        queries,
        residual_in,
        key_new,
        value_new,
        key_cache,
        value_cache,
        cache_lens,
        norm_gain.reshape(1, D),
        expert_ids.T,
        gate_weights.T,
        w_in,
        w_out,
    )
    return (attended.astype(BF), expert_mix.astype(BF))


def solution(mesh):
    return jax.shard_map(
        body,
        mesh=mesh,
        in_specs=(
            P(("pool", "grp"), "cuts"),
            P(("pool", "grp"), "cuts"),
            P(("pool", "grp"), "cuts"),
            P(("pool", "grp"), "cuts"),
            P(("pool", "grp"), None, "cuts"),
            P(("pool", "grp"), None, "cuts"),
            P(("pool", "grp")),
            P(),
            P(("pool", "grp"), None),
            P(("pool", "grp"), None),
            P("grp", None, ("pool", "cuts")),
            P("grp", ("pool", "cuts"), None),
        ),
        out_specs=(P(("pool", "grp"), "cuts"), P(("pool", "grp"), "cuts")),
        check_vma=False,
    )
```

```python
import math

import jax
import jax.numpy as jnp
from jax import lax
from jax.experimental import pallas as pl
from jax.experimental.pallas import tpu as pltpu
from jax.sharding import PartitionSpec as P

MESH = pl.DeviceIdType.MESH
BF, F32 = jnp.bfloat16, jnp.float32
OFFS = (0, 1, 7, 3, 5, 4, 2, 6)
UNITS = 8
UR = 64
ALL = UNITS * UR
SLOTS = 16
CW = 768
CUTS = 8
FF = 384
D = CUTS * CW
ROWS = 32
HEADS = 6
SPAN = 128
HD = 128
N_SEND = 14
N_RECV = 80
PLAN = (
    ("sx", 1), ("sx", 3), ("sx", 0), ("x", 1), ("z", 1), ("sx", 2), ("x", 3), ("z", 2), ("z", 3),
    ("z", 4), ("x", 0), ("a0", 0), ("a0", 1), ("a0", 2), ("a1", 1), ("x", 2), ("z", 5), ("z", 6),
    ("a1", 0), ("a1", 2), ("a0", 3), ("a2", 1), ("a2", 0), ("a0", 4), ("z", 7), ("a1", 3),
    ("a0", 5), ("mm", (0, 1)), ("a0", 6), ("a2", 2), ("a2", 3), ("b0", (0,)), ("b0", (1,)),
    ("a1", 4), ("a1", 5), ("a0", 7), ("mm", (2, 3)), ("b0", (2, 3)), ("a2", 4), ("a1", 6),
    ("b1", (2, 3)), ("a2", 5), ("b1", (1,)), ("mm", (4, 5)), ("a1", 7), ("b0", (4, 5)),
    ("b1", (4, 5)), ("b2", (2, 3)), ("b2", (4, 5)), ("a2", 6), ("a2", 7), ("mm", (6, 7)),
    ("b1", (0,)), ("b3", (2, 3)), ("b0", (6, 7)), ("b1", (6, 7)), ("b2", (1,)), ("b3", (4, 5)),
    ("b2", (6, 7)), ("b2", (0,)), ("b3", (1,)), ("b3", (6, 7)), ("b3", (0,)), ("b4", 3),
    ("b4", 0), ("b4", 1), ("b4", 2),
)
FIRST_MM = (0, 1)
FIRST_B0 = (0,)


def dot(a, b):
    return jnp.dot(a, b, preferred_element_type=F32)


def attention(q, knew, vnew, lens, kbuf, vbuf, kv_loads, q3, s3, o3):
    scale = 1.0 / math.sqrt(HD)
    q3[...] = jnp.zeros(q3.shape, F32)
    for h in range(HEADS):
        q3[:, h, :] = q[:, h * HD : (h + 1) * HD].astype(F32)
    new_k, new_v = knew[...].astype(F32), vnew[...].astype(F32)
    lane = lax.broadcasted_iota(jnp.int32, (8, SPAN), 1)
    for w in kv_loads[: len(kv_loads) // 2]:
        w.wait()
    own = []
    for r in range(ROWS):
        qr = q3[r]
        s = lax.dot_general(
            qr.astype(BF), kbuf[r], (((1,), (1,)), ((), ())), preferred_element_type=F32
        )
        s3[r] = jnp.where(lane < lens[r], s * scale, -1e30)
        own.append(jnp.sum(qr * new_k[r : r + 1, :], axis=1, keepdims=True) * scale)
    for w in kv_loads[len(kv_loads) // 2 :]:
        w.wait()
    for r in range(ROWS):
        s = s3[r]
        peak = jnp.maximum(jnp.max(s, axis=1, keepdims=True), own[r])
        raw = jnp.where(lane < lens[r], jnp.exp(s - peak), 0.0)
        own_raw = jnp.exp(own[r] - peak)
        total = jnp.sum(raw, axis=1, keepdims=True) + own_raw
        probs = (raw / total).astype(BF)
        own_prob = (own_raw / total).astype(BF).astype(F32)
        o3[r] = dot(probs, vbuf[r]) + own_prob * new_v[r : r + 1, :]


def routing(ids, gates, x, zl):
    j = lax.broadcasted_iota(jnp.int32, (16, ROWS), 0)
    expert = (((zl + (j & 3)) & 3) << 2) + ((x + (j >> 2)) & 3)
    chosen = jnp.zeros((16, ROWS), F32)
    weight = jnp.zeros((16, ROWS), F32)
    for t in range(4):
        hit = ids[t : t + 1, :] == expert
        chosen = chosen + jnp.where(hit, 1.0, 0.0)
        weight = weight + jnp.where(hit, gates[t : t + 1, :], 0.0)
    before = lax.broadcasted_iota(jnp.int32, (ROWS, ROWS), 0) < lax.broadcasted_iota(
        jnp.int32, (ROWS, ROWS), 1
    )
    slot = dot(chosen.astype(BF), jnp.where(before, 1.0, 0.0).astype(BF))
    spread = (lax.broadcasted_iota(jnp.int32, (256, 16), 0) >> 4) == (
        lax.broadcasted_iota(jnp.int32, (256, 16), 1)
    )
    spread = jnp.where(spread, 1.0, 0.0).astype(BF)
    high = weight.astype(BF)
    low = (weight - high.astype(F32)).astype(BF)
    place = (lax.broadcasted_iota(jnp.int32, (256, ROWS), 0) & 15).astype(F32)
    here = (dot(spread, chosen.astype(BF)) > 0.5) & (dot(spread, slot.astype(BF)) == place)
    disp = jnp.where(here, 1.0, 0.0).astype(BF)
    high = jnp.where(here, dot(spread, high), 0.0).T.astype(BF)
    low = jnp.where(here, dot(spread, low), 0.0).T.astype(BF)
    return disp, high, low


def moe_kernel(
    q, res, knew, vnew, kc, vc, lens, gain, ids, gates, w_in, w_out, out, att_out,
    kbuf, vbuf, q3, s3, o3, xout, xbuf, big, win, wout, acc, hid, sib_out, sib_in, far, fwd,
    step_a, step_b, sum_a, sum_b, done, home_z, pair, home_x,
    send_sem, recv_sem, local_sem,
):
    pool, grp, cuts = lax.axis_index("pool"), lax.axis_index("grp"), lax.axis_index("cuts")
    zl, x = grp // 4, grp % 4
    z = pool * 4 + zl
    y, k = cuts // 2, cuts % 2

    def at_z(off):
        t = (z + off) % 8
        return (t // 4, (t % 4) * 4 + x, cuts)

    def at_x(off):
        return (pool, zl * 4 + (x + off) % 4, cuts)

    sibling = (pool, grp, y * 2 + (1 - k))
    up = (pool, grp, (cuts + 2) % 8)
    down = (pool, grp, (cuts + 6) % 8)

    ys = (0, 3, 1, 2)

    def cut_of(s):
        core = k if s < 4 else 1 - k
        return ((y + ys[s % 4]) % 4) * 2 + core

    def load(src, dst, i):
        copy = pltpu.make_async_copy(src, dst, local_sem.at[i])
        copy.start()
        return copy

    kv_loads = [load(kc, kbuf, 0), load(vc, vbuf, 1)]

    barrier = pltpu.get_barrier_semaphore()
    peers = [sibling, up, down]
    peers += [at_x(o) for o in range(1, 4)]
    peers += [at_z(o) for o in range(1, 8)]
    for peer in peers:
        pl.semaphore_signal(barrier, inc=1, device_id=peer, device_id_type=MESH)

    sends, arrivals = {}, {}

    def push(src, dst, where, stream, arrival):
        rows = math.prod(src.shape[:-1])
        out_at = sends.setdefault(stream, [len(sends), 0])
        in_at = arrivals.setdefault(arrival, [len(arrivals), 0])
        out_at[1] += rows
        in_at[1] += rows
        pltpu.make_async_remote_copy(
            src_ref=src,
            dst_ref=dst,
            send_sem=send_sem.at[out_at[0]],
            recv_sem=recv_sem.at[in_at[0]],
            device_id=where,
            device_id_type=MESH,
        ).start()

    def block_of(rows):
        return big.at[0, pl.ds(0, rows)] if rows <= ALL else sib_out.at[pl.ds(0, rows // ALL)]

    def arrived(key):
        at, rows = arrivals[key]
        pltpu.make_async_copy(block_of(rows), block_of(rows), recv_sem.at[at]).wait()

    disp, high, low = routing(ids, gates, x, zl)
    attention(q, knew, vnew, lens, kbuf, vbuf, kv_loads, q3, s3, o3)
    for s in range(CUTS):
        load(w_in.at[0, pl.ds(pl.multiple_of(cut_of(s) * CW, CW), CW), :], win.at[s], 2)
    for s in range(CUTS):
        load(w_out.at[0, :, pl.ds(pl.multiple_of(cut_of(s) * CW, CW), CW)], wout.at[s], 3)
    for h in range(HEADS):
        att_out[:, h * HD : (h + 1) * HD] = o3[:, h, :].astype(BF).astype(F32)
    stream = (res[...].astype(F32) + att_out[...]).astype(BF)

    blocks = dot(disp, stream).astype(BF)
    pl.semaphore_wait(barrier, len(peers))

    def start_x(d):
        for r in range(4):
            block = blocks[(r * 4 + d) * SLOTS : (r * 4 + d + 1) * SLOTS]
            if r == 0:
                xbuf[d, 0:SLOTS, :] = block
            else:
                xout[d, r] = block
        for r in (2, 1, 3):
            push(
                xout.at[d, r], xbuf.at[d, pl.ds(r * SLOTS, SLOTS), :], at_x(r), "x", ("x", d)
            )

    def rows_of(units):
        return units[0] * UR, len(units) * UR

    def stage_x(d):
        arrived(("x", d))
        if d == 0:
            big[0, 0:UR] = xbuf[0]

    def stage_z(u):
        push(xbuf.at[OFFS[u] % 4], big.at[0, pl.ds(u * UR, UR)], at_z(OFFS[u]), "z", ("z", u))

    def to_sibling(i, u):
        at = pl.ds(u * UR, UR)
        push(big.at[i, at], big.at[4 + i, at], sibling, "s", ("s", u // 2))

    def stage_a0(u):
        if OFFS[u] != 0:
            arrived(("z", u))
        at = pl.ds(u * UR, UR)
        push(big.at[0, at], big.at[1, at], up, "u", ("u", u))
        push(big.at[0, at], big.at[2, at], down, "d", ("d", u))
        to_sibling(0, u)

    def stage_a1(u):
        top, bottom = pl.ds(u * UR, 32), pl.ds(u * UR + 32, 32)
        arrived(("u", u))
        push(big.at[1, top], big.at[3, top], up, "f", ("f", u))
        to_sibling(1, u)
        arrived(("d", u))
        push(big.at[2, bottom], big.at[3, bottom], down, "g", ("f", u))
        to_sibling(2, u)

    def stage_a2(u):
        arrived(("f", u))
        to_sibling(3, u)

    def stage_mm(units):
        if units == FIRST_MM:
            pltpu.make_async_copy(win, win, local_sem.at[2]).wait()
        arrived(("s", units[0] // 2))
        base, n = rows_of(units)
        at = slice(base, base + n)

        def add_stats(s, sums):
            total, squares = sums
            rows = big[s, at, :].astype(F32)
            for l in range(CW // 128):
                v = rows[:, l * 128 : (l + 1) * 128]
                total = total + v
                squares = squares + v * v
            return total, squares

        zero = jnp.zeros((n, 128), F32)
        total, squares = lax.fori_loop(0, CUTS, add_stats, (zero, zero))
        mean = jnp.sum(total, axis=1, keepdims=True) * (1.0 / D)
        variance = jnp.sum(squares, axis=1, keepdims=True) * (1.0 / D) - mean * mean
        scale = lax.rsqrt(variance + 1e-05)
        for s in range(CUTS):
            rows = big[s, at, :].astype(F32)
            factor = gain[:, pl.ds(pl.multiple_of(cut_of(s) * CW, CW), CW)]
            normed = ((rows - mean) * scale * factor).astype(BF)
            part = dot(normed, win[s])
            if s == 0:
                acc[0:n] = part
            elif s < CUTS - 1:
                acc[0:n] += part
        inner = acc[0:n] + part
        hid[at, :] = (inner / (1.0 + jnp.exp(-inner))).astype(BF)

    def stage_b0(units):
        if units == FIRST_B0:
            pltpu.make_async_copy(wout, wout, local_sem.at[3]).wait()
        base, n = rows_of(units)
        at = pl.ds(base, n)
        mine = hid[base : base + n]
        for i in (3, 2, 1, 0):
            sib_out[i, at] = dot(mine, wout[4 + i]).astype(BF)
            push(sib_out.at[i, at], sib_in.at[i, at], sibling, "b", ("b", units, i))

    def chip_sum(units, i):
        base, n = rows_of(units)
        part = dot(hid[base : base + n], wout[i])
        arrived(("b", units, i))
        return part + sib_in[i, base : base + n].astype(F32)

    def stage_b1(units):
        base, n = rows_of(units)
        h = n // 2
        far[base : base + n] = chip_sum(units, 3).astype(BF)
        top, bottom = pl.ds(base, h), pl.ds(base + h, h)
        push(far.at[top], fwd.at[top], up, "fa", ("fa", units))
        push(far.at[bottom], fwd.at[bottom], down, "fb", ("fb", units))

    def stage_b2(units):
        base, n = rows_of(units)
        h, at = n // 2, pl.ds(base, n)
        part = chip_sum(units, 2)
        arrived(("fa", units))
        sum_a[base : base + h] = (part[0:h] + fwd[base : base + h].astype(F32)).astype(BF)
        sum_a[base + h : base + n] = part[h:n].astype(BF)
        push(sum_a.at[at], step_a.at[at], up, "ga", ("g", units))
        part = chip_sum(units, 1)
        arrived(("fb", units))
        sum_b[base : base + h] = part[0:h].astype(BF)
        sum_b[base + h : base + n] = (
            part[h:n] + fwd[base + h : base + n].astype(F32)
        ).astype(BF)
        push(sum_b.at[at], step_b.at[at], down, "gb", ("g", units))

    def stage_b3(units):
        base, n = rows_of(units)
        part = chip_sum(units, 0)
        arrived(("g", units))
        part = part + step_a[base : base + n].astype(F32) + step_b[base : base + n].astype(F32)
        part = part.astype(BF)
        for i, u in enumerate(units):
            half = part[i * UR : (i + 1) * UR]
            if OFFS[u] == 0:
                home_z[u] = half
            else:
                done[u] = half
                push(done.at[u], home_z.at[u], at_z(8 - OFFS[u]), "h", ("h", OFFS[u] % 4))

    def stage_b4(d):
        units = [u for u in range(UNITS) if OFFS[u] % 4 == d]
        arrived(("h", d))
        both = home_z[units[0]].astype(F32) + home_z[units[1]].astype(F32)
        both = both.astype(BF)
        home_x[0, d] = both[0:SLOTS]
        pair[d] = both
        for r in (2, 1, 3):
            push(
                pair.at[d, pl.ds(r * SLOTS, SLOTS), :], home_x.at[r, d], at_x(4 - r), "hx", "hx"
            )

    stages = {
        "sx": start_x, "x": stage_x, "z": stage_z, "a0": stage_a0, "a1": stage_a1, "a2": stage_a2,
        "mm": stage_mm, "b0": stage_b0, "b1": stage_b1, "b2": stage_b2, "b3": stage_b3,
        "b4": stage_b4,
    }
    for name, i in PLAN:
        stages[name](i)

    arrived("hx")
    back = home_x[...].reshape(4 * 4 * SLOTS, CW)
    out[...] = dot(high, back) + dot(low, back)
    for at, rows in sends.values():
        pltpu.make_async_copy(block_of(rows), block_of(rows), send_sem.at[at]).wait()


def body(
    residual_in,
    queries,
    key_new,
    value_new,
    key_cache,
    value_cache,
    cache_lens,
    norm_gain,
    expert_ids,
    gate_weights,
    w_in,
    w_out,
):
    vmem = pl.BlockSpec(memory_space=pltpu.VMEM)
    smem = pl.BlockSpec(memory_space=pltpu.SMEM)
    hbm = pl.BlockSpec(memory_space=pl.ANY)
    expert_mix, attended = pl.pallas_call(
        moe_kernel,
        out_shape=(
            jax.ShapeDtypeStruct((ROWS, CW), F32),
            jax.ShapeDtypeStruct((ROWS, CW), F32),
        ),
        in_specs=[vmem] * 4 + [hbm] * 2 + [smem] + [vmem] * 3 + [hbm] * 2,
        out_specs=(vmem, vmem),
        scratch_shapes=[
            pltpu.VMEM((ROWS, SPAN, HD), BF),
            pltpu.VMEM((ROWS, SPAN, HD), BF),
            pltpu.VMEM((ROWS, 8, HD), F32),
            pltpu.VMEM((ROWS, 8, SPAN), F32),
            pltpu.VMEM((ROWS, 8, HD), F32),
            pltpu.VMEM((4, 4, SLOTS, CW), BF),
            pltpu.VMEM((4, UR, CW), BF),
            pltpu.VMEM((CUTS, ALL, CW), BF),
            pltpu.VMEM((CUTS, CW, FF), BF),
            pltpu.VMEM((CUTS, FF, CW), BF),
            pltpu.VMEM((2 * UR, FF), F32),
            pltpu.VMEM((ALL, FF), BF),
            pltpu.VMEM((4, ALL, CW), BF),
            pltpu.VMEM((4, ALL, CW), BF),
            pltpu.VMEM((ALL, CW), BF),
            pltpu.VMEM((ALL, CW), BF),
            pltpu.VMEM((ALL, CW), BF),
            pltpu.VMEM((ALL, CW), BF),
            pltpu.VMEM((ALL, CW), BF),
            pltpu.VMEM((ALL, CW), BF),
            pltpu.VMEM((UNITS, UR, CW), BF),
            pltpu.VMEM((UNITS, UR, CW), BF),
            pltpu.VMEM((4, UR, CW), BF),
            pltpu.VMEM((4, 4, SLOTS, CW), BF),
            pltpu.SemaphoreType.DMA((N_SEND,)),
            pltpu.SemaphoreType.DMA((N_RECV,)),
            pltpu.SemaphoreType.DMA((4,)),
        ],
        compiler_params=pltpu.CompilerParams(
            collective_id=0, has_side_effects=True, vmem_limit_bytes=56 * 1024 * 1024
        ),
    )(
        queries,
        residual_in,
        key_new,
        value_new,
        key_cache,
        value_cache,
        cache_lens,
        norm_gain.reshape(1, D),
        expert_ids.T,
        gate_weights.T,
        w_in,
        w_out,
    )
    return (attended.astype(BF), expert_mix.astype(BF))


def solution(mesh):
    return jax.shard_map(
        body,
        mesh=mesh,
        in_specs=(
            P(("pool", "grp"), "cuts"),
            P(("pool", "grp"), "cuts"),
            P(("pool", "grp"), "cuts"),
            P(("pool", "grp"), "cuts"),
            P(("pool", "grp"), None, "cuts"),
            P(("pool", "grp"), None, "cuts"),
            P(("pool", "grp")),
            P(),
            P(("pool", "grp"), None),
            P(("pool", "grp"), None),
            P("grp", None, ("pool", "cuts")),
            P("grp", ("pool", "cuts"), None),
        ),
        out_specs=(P(("pool", "grp"), "cuts"), P(("pool", "grp"), "cuts")),
        check_vma=False,
    )
```

```python
import math

import jax
import jax.numpy as jnp
from jax import lax
from jax.experimental import pallas as pl
from jax.experimental.pallas import tpu as pltpu
from jax.sharding import PartitionSpec as P

MESH = pl.DeviceIdType.MESH
BF, F32 = jnp.bfloat16, jnp.float32
OFFS = (0, 1, 7, 3, 5, 4, 2, 6)
UNITS = 8
UR = 64
ALL = UNITS * UR
SLOTS = 16
CW = 768
CUTS = 8
FF = 384
D = CUTS * CW
ROWS = 32
HEADS = 6
SPAN = 128
HD = 128
N_SEND = 14
N_RECV = 80
PLAN = (
    ("sx", 3), ("sx", 0), ("sx", 1), ("x", 3), ("z", 2), ("z", 3), ("x", 0), ("a0", 0), ("x", 1),
    ("z", 4), ("a0", 2), ("z", 1), ("sx", 2), ("z", 5), ("a1", 0), ("a1", 2), ("a0", 3), ("x", 2),
    ("a0", 4), ("z", 6), ("z", 7), ("a1", 3), ("a0", 1), ("a1", 4), ("a0", 5), ("a2", 3),
    ("a2", 2), ("a0", 6), ("mm", (2, 3)), ("a1", 5), ("b0", (2, 3)), ("a0", 7), ("a1", 1),
    ("a2", 4), ("b1", (2, 3)), ("a2", 0), ("a1", 6), ("a2", 5), ("mm", (4, 5)), ("a1", 7),
    ("b0", (4, 5)), ("a2", 1), ("b1", (4, 5)), ("b2", (2, 3)), ("a2", 6), ("mm", (0, 1)),
    ("a2", 7), ("b0", (0,)), ("b2", (4, 5)), ("mm", (6, 7)), ("b0", (1,)), ("b0", (6, 7)),
    ("b1", (1,)), ("b3", (2, 3)), ("b1", (6, 7)), ("b3", (4, 5)), ("b2", (1,)), ("b2", (6, 7)),
    ("b4", 3), ("b3", (1,)), ("b1", (0,)), ("b3", (6, 7)), ("b2", (0,)), ("b4", 1), ("b3", (0,)),
    ("b4", 0), ("b4", 2),
)
FIRST_MM = (2, 3)
FIRST_B0 = (2, 3)


def dot(a, b):
    return jnp.dot(a, b, preferred_element_type=F32)


def attention(q, knew, vnew, lens, kbuf, vbuf, kv_loads, q3, s3, o3):
    scale = 1.0 / math.sqrt(HD)
    q3[...] = jnp.zeros(q3.shape, F32)
    for h in range(HEADS):
        q3[:, h, :] = q[:, h * HD : (h + 1) * HD].astype(F32)
    new_k, new_v = knew[...].astype(F32), vnew[...].astype(F32)
    lane = lax.broadcasted_iota(jnp.int32, (8, SPAN), 1)
    for w in kv_loads[: len(kv_loads) // 2]:
        w.wait()
    own = []
    for r in range(ROWS):
        qr = q3[r]
        s = lax.dot_general(
            qr.astype(BF), kbuf[r], (((1,), (1,)), ((), ())), preferred_element_type=F32
        )
        s3[r] = jnp.where(lane < lens[r], s * scale, -1e30)
        own.append(jnp.sum(qr * new_k[r : r + 1, :], axis=1, keepdims=True) * scale)
    for w in kv_loads[len(kv_loads) // 2 :]:
        w.wait()
    for r in range(ROWS):
        s = s3[r]
        peak = jnp.maximum(jnp.max(s, axis=1, keepdims=True), own[r])
        raw = jnp.where(lane < lens[r], jnp.exp(s - peak), 0.0)
        own_raw = jnp.exp(own[r] - peak)
        total = jnp.sum(raw, axis=1, keepdims=True) + own_raw
        probs = (raw / total).astype(BF)
        own_prob = (own_raw / total).astype(BF).astype(F32)
        o3[r] = dot(probs, vbuf[r]) + own_prob * new_v[r : r + 1, :]


def routing(ids, gates, x, zl):
    j = lax.broadcasted_iota(jnp.int32, (16, ROWS), 0)
    expert = (((zl + (j & 3)) & 3) << 2) + ((x + (j >> 2)) & 3)
    chosen = jnp.zeros((16, ROWS), F32)
    weight = jnp.zeros((16, ROWS), F32)
    for t in range(4):
        hit = ids[t : t + 1, :] == expert
        chosen = chosen + jnp.where(hit, 1.0, 0.0)
        weight = weight + jnp.where(hit, gates[t : t + 1, :], 0.0)
    before = lax.broadcasted_iota(jnp.int32, (ROWS, ROWS), 0) < lax.broadcasted_iota(
        jnp.int32, (ROWS, ROWS), 1
    )
    slot = dot(chosen.astype(BF), jnp.where(before, 1.0, 0.0).astype(BF))
    spread = (lax.broadcasted_iota(jnp.int32, (256, 16), 0) >> 4) == (
        lax.broadcasted_iota(jnp.int32, (256, 16), 1)
    )
    spread = jnp.where(spread, 1.0, 0.0).astype(BF)
    high = weight.astype(BF)
    low = (weight - high.astype(F32)).astype(BF)
    place = (lax.broadcasted_iota(jnp.int32, (256, ROWS), 0) & 15).astype(F32)
    here = (dot(spread, chosen.astype(BF)) > 0.5) & (dot(spread, slot.astype(BF)) == place)
    disp = jnp.where(here, 1.0, 0.0).astype(BF)
    high = jnp.where(here, dot(spread, high), 0.0).T.astype(BF)
    low = jnp.where(here, dot(spread, low), 0.0).T.astype(BF)
    return disp, high, low


def moe_kernel(
    q, res, knew, vnew, kc, vc, lens, gain, ids, gates, w_in, w_out, out, att_out,
    kbuf, vbuf, q3, s3, o3, xout, xbuf, big, win, wout, acc, hid, sib_out, sib_in, far, fwd,
    step_a, step_b, sum_a, sum_b, done, home_z, pair, home_x,
    send_sem, recv_sem, local_sem,
):
    pool, grp, cuts = lax.axis_index("pool"), lax.axis_index("grp"), lax.axis_index("cuts")
    zl, x = grp // 4, grp % 4
    z = pool * 4 + zl
    y, k = cuts // 2, cuts % 2

    def at_z(off):
        t = (z + off) % 8
        return (t // 4, (t % 4) * 4 + x, cuts)

    def at_x(off):
        return (pool, zl * 4 + (x + off) % 4, cuts)

    sibling = (pool, grp, y * 2 + (1 - k))
    up = (pool, grp, (cuts + 2) % 8)
    down = (pool, grp, (cuts + 6) % 8)

    ys = (0, 3, 1, 2)

    def cut_of(s):
        core = k if s < 4 else 1 - k
        return ((y + ys[s % 4]) % 4) * 2 + core

    def load(src, dst, i):
        copy = pltpu.make_async_copy(src, dst, local_sem.at[i])
        copy.start()
        return copy

    kv_loads = [load(kc, kbuf, 0), load(vc, vbuf, 1)]

    barrier = pltpu.get_barrier_semaphore()
    peers = [sibling, up, down]
    peers += [at_x(o) for o in range(1, 4)]
    peers += [at_z(o) for o in range(1, 8)]
    for peer in peers:
        pl.semaphore_signal(barrier, inc=1, device_id=peer, device_id_type=MESH)

    sends, arrivals = {}, {}

    def push(src, dst, where, stream, arrival):
        rows = math.prod(src.shape[:-1])
        out_at = sends.setdefault(stream, [len(sends), 0])
        in_at = arrivals.setdefault(arrival, [len(arrivals), 0])
        out_at[1] += rows
        in_at[1] += rows
        pltpu.make_async_remote_copy(
            src_ref=src,
            dst_ref=dst,
            send_sem=send_sem.at[out_at[0]],
            recv_sem=recv_sem.at[in_at[0]],
            device_id=where,
            device_id_type=MESH,
        ).start()

    def block_of(rows):
        return big.at[0, pl.ds(0, rows)] if rows <= ALL else sib_out.at[pl.ds(0, rows // ALL)]

    def arrived(key):
        at, rows = arrivals[key]
        pltpu.make_async_copy(block_of(rows), block_of(rows), recv_sem.at[at]).wait()

    disp, high, low = routing(ids, gates, x, zl)
    attention(q, knew, vnew, lens, kbuf, vbuf, kv_loads, q3, s3, o3)
    for s in range(CUTS):
        load(w_in.at[0, pl.ds(pl.multiple_of(cut_of(s) * CW, CW), CW), :], win.at[s], 2)
    for s in range(CUTS):
        load(w_out.at[0, :, pl.ds(pl.multiple_of(cut_of(s) * CW, CW), CW)], wout.at[s], 3)
    for h in range(HEADS):
        att_out[:, h * HD : (h + 1) * HD] = o3[:, h, :].astype(BF)
    stream = (res[...].astype(F32) + att_out[...].astype(F32)).astype(BF)

    blocks = dot(disp, stream).astype(BF)
    pl.semaphore_wait(barrier, len(peers))

    def start_x(d):
        for r in range(4):
            block = blocks[(r * 4 + d) * SLOTS : (r * 4 + d + 1) * SLOTS]
            if r == 0:
                xbuf[d, 0:SLOTS, :] = block
            else:
                xout[d, r] = block
        for r in (2, 1, 3):
            push(
                xout.at[d, r], xbuf.at[d, pl.ds(r * SLOTS, SLOTS), :], at_x(r), "x", ("x", d)
            )

    def rows_of(units):
        return units[0] * UR, len(units) * UR

    def stage_x(d):
        arrived(("x", d))
        if d == 0:
            big[0, 0:UR] = xbuf[0]

    def stage_z(u):
        push(xbuf.at[OFFS[u] % 4], big.at[0, pl.ds(u * UR, UR)], at_z(OFFS[u]), "z", ("z", u))

    def to_sibling(i, u):
        at = pl.ds(u * UR, UR)
        push(big.at[i, at], big.at[4 + i, at], sibling, "s", ("s", u // 2))

    def stage_a0(u):
        if OFFS[u] != 0:
            arrived(("z", u))
        at = pl.ds(u * UR, UR)
        push(big.at[0, at], big.at[1, at], up, "u", ("u", u))
        push(big.at[0, at], big.at[2, at], down, "d", ("d", u))
        to_sibling(0, u)

    def stage_a1(u):
        top, bottom = pl.ds(u * UR, 32), pl.ds(u * UR + 32, 32)
        arrived(("u", u))
        push(big.at[1, top], big.at[3, top], up, "f", ("f", u))
        to_sibling(1, u)
        arrived(("d", u))
        push(big.at[2, bottom], big.at[3, bottom], down, "g", ("f", u))
        to_sibling(2, u)

    def stage_a2(u):
        arrived(("f", u))
        to_sibling(3, u)

    def stage_mm(units):
        if units == FIRST_MM:
            pltpu.make_async_copy(win, win, local_sem.at[2]).wait()
        arrived(("s", units[0] // 2))
        base, n = rows_of(units)
        at = slice(base, base + n)

        def add_stats(s, sums):
            total, squares = sums
            rows = big[s, at, :].astype(F32)
            for l in range(CW // 128):
                v = rows[:, l * 128 : (l + 1) * 128]
                total = total + v
                squares = squares + v * v
            return total, squares

        zero = jnp.zeros((n, 128), F32)
        total, squares = lax.fori_loop(0, CUTS, add_stats, (zero, zero))
        mean = jnp.sum(total, axis=1, keepdims=True) * (1.0 / D)
        variance = jnp.sum(squares, axis=1, keepdims=True) * (1.0 / D) - mean * mean
        scale = lax.rsqrt(variance + 1e-05)
        for s in range(CUTS):
            rows = big[s, at, :].astype(F32)
            factor = gain[:, pl.ds(pl.multiple_of(cut_of(s) * CW, CW), CW)]
            normed = ((rows - mean) * scale * factor).astype(BF)
            part = dot(normed, win[s])
            if s == 0:
                acc[0:n] = part
            elif s < CUTS - 1:
                acc[0:n] += part
        inner = acc[0:n] + part
        hid[at, :] = (inner / (1.0 + jnp.exp(-inner))).astype(BF)

    def stage_b0(units):
        if units == FIRST_B0:
            pltpu.make_async_copy(wout, wout, local_sem.at[3]).wait()
        base, n = rows_of(units)
        at = pl.ds(base, n)
        mine = hid[base : base + n]
        for i in (3, 2, 1, 0):
            sib_out[i, at] = dot(mine, wout[4 + i]).astype(BF)
            push(sib_out.at[i, at], sib_in.at[i, at], sibling, "b", ("b", units, i))

    def chip_sum(units, i):
        base, n = rows_of(units)
        part = dot(hid[base : base + n], wout[i])
        arrived(("b", units, i))
        return part + sib_in[i, base : base + n].astype(F32)

    def stage_b1(units):
        base, n = rows_of(units)
        h = n // 2
        far[base : base + n] = chip_sum(units, 3).astype(BF)
        top, bottom = pl.ds(base, h), pl.ds(base + h, h)
        push(far.at[top], fwd.at[top], up, "fa", ("fa", units))
        push(far.at[bottom], fwd.at[bottom], down, "fb", ("fb", units))

    def stage_b2(units):
        base, n = rows_of(units)
        h, at = n // 2, pl.ds(base, n)
        part = chip_sum(units, 2)
        arrived(("fa", units))
        sum_a[base : base + h] = (part[0:h] + fwd[base : base + h].astype(F32)).astype(BF)
        sum_a[base + h : base + n] = part[h:n].astype(BF)
        push(sum_a.at[at], step_a.at[at], up, "ga", ("g", units))
        part = chip_sum(units, 1)
        arrived(("fb", units))
        sum_b[base : base + h] = part[0:h].astype(BF)
        sum_b[base + h : base + n] = (
            part[h:n] + fwd[base + h : base + n].astype(F32)
        ).astype(BF)
        push(sum_b.at[at], step_b.at[at], down, "gb", ("g", units))

    def stage_b3(units):
        base, n = rows_of(units)
        part = chip_sum(units, 0)
        arrived(("g", units))
        part = part + step_a[base : base + n].astype(F32) + step_b[base : base + n].astype(F32)
        part = part.astype(BF)
        for i, u in enumerate(units):
            half = part[i * UR : (i + 1) * UR]
            if OFFS[u] == 0:
                home_z[u] = half
            else:
                done[u] = half
                push(done.at[u], home_z.at[u], at_z(8 - OFFS[u]), "h", ("h", OFFS[u] % 4))

    def stage_b4(d):
        units = [u for u in range(UNITS) if OFFS[u] % 4 == d]
        arrived(("h", d))
        both = home_z[units[0]].astype(F32) + home_z[units[1]].astype(F32)
        both = both.astype(BF)
        home_x[0, d] = both[0:SLOTS]
        pair[d] = both
        for r in (2, 1, 3):
            push(
                pair.at[d, pl.ds(r * SLOTS, SLOTS), :], home_x.at[r, d], at_x(4 - r), "hx", "hx"
            )

    stages = {
        "sx": start_x, "x": stage_x, "z": stage_z, "a0": stage_a0, "a1": stage_a1, "a2": stage_a2,
        "mm": stage_mm, "b0": stage_b0, "b1": stage_b1, "b2": stage_b2, "b3": stage_b3,
        "b4": stage_b4,
    }
    for name, i in PLAN:
        stages[name](i)

    arrived("hx")
    back = home_x[...].reshape(4 * 4 * SLOTS, CW)
    out[...] = (dot(high, back) + dot(low, back)).astype(BF)
    for at, rows in sends.values():
        pltpu.make_async_copy(block_of(rows), block_of(rows), send_sem.at[at]).wait()


def body(
    residual_in,
    queries,
    key_new,
    value_new,
    key_cache,
    value_cache,
    cache_lens,
    norm_gain,
    expert_ids,
    gate_weights,
    w_in,
    w_out,
):
    vmem = pl.BlockSpec(memory_space=pltpu.VMEM)
    smem = pl.BlockSpec(memory_space=pltpu.SMEM)
    hbm = pl.BlockSpec(memory_space=pl.ANY)
    expert_mix, attended = pl.pallas_call(
        moe_kernel,
        out_shape=(
            jax.ShapeDtypeStruct((ROWS, CW), BF),
            jax.ShapeDtypeStruct((ROWS, CW), BF),
        ),
        in_specs=[vmem] * 4 + [hbm] * 2 + [smem] + [vmem] * 3 + [hbm] * 2,
        out_specs=(vmem, vmem),
        scratch_shapes=[
            pltpu.VMEM((ROWS, SPAN, HD), BF),
            pltpu.VMEM((ROWS, SPAN, HD), BF),
            pltpu.VMEM((ROWS, 8, HD), F32),
            pltpu.VMEM((ROWS, 8, SPAN), F32),
            pltpu.VMEM((ROWS, 8, HD), F32),
            pltpu.VMEM((4, 4, SLOTS, CW), BF),
            pltpu.VMEM((4, UR, CW), BF),
            pltpu.VMEM((CUTS, ALL, CW), BF),
            pltpu.VMEM((CUTS, CW, FF), BF),
            pltpu.VMEM((CUTS, FF, CW), BF),
            pltpu.VMEM((2 * UR, FF), F32),
            pltpu.VMEM((ALL, FF), BF),
            pltpu.VMEM((4, ALL, CW), BF),
            pltpu.VMEM((4, ALL, CW), BF),
            pltpu.VMEM((ALL, CW), BF),
            pltpu.VMEM((ALL, CW), BF),
            pltpu.VMEM((ALL, CW), BF),
            pltpu.VMEM((ALL, CW), BF),
            pltpu.VMEM((ALL, CW), BF),
            pltpu.VMEM((ALL, CW), BF),
            pltpu.VMEM((UNITS, UR, CW), BF),
            pltpu.VMEM((UNITS, UR, CW), BF),
            pltpu.VMEM((4, UR, CW), BF),
            pltpu.VMEM((4, 4, SLOTS, CW), BF),
            pltpu.SemaphoreType.DMA((N_SEND,)),
            pltpu.SemaphoreType.DMA((N_RECV,)),
            pltpu.SemaphoreType.DMA((4,)),
        ],
        compiler_params=pltpu.CompilerParams(
            collective_id=0, has_side_effects=True, vmem_limit_bytes=56 * 1024 * 1024
        ),
    )(
        queries,
        residual_in,
        key_new,
        value_new,
        key_cache,
        value_cache,
        cache_lens,
        norm_gain.reshape(1, D),
        expert_ids.T,
        gate_weights.T,
        w_in,
        w_out,
    )
    return (attended, expert_mix)


def solution(mesh):
    return jax.shard_map(
        body,
        mesh=mesh,
        in_specs=(
            P(("pool", "grp"), "cuts"),
            P(("pool", "grp"), "cuts"),
            P(("pool", "grp"), "cuts"),
            P(("pool", "grp"), "cuts"),
            P(("pool", "grp"), None, "cuts"),
            P(("pool", "grp"), None, "cuts"),
            P(("pool", "grp")),
            P(),
            P(("pool", "grp"), None),
            P(("pool", "grp"), None),
            P("grp", None, ("pool", "cuts")),
            P("grp", ("pool", "cuts"), None),
        ),
        out_specs=(P(("pool", "grp"), "cuts"), P(("pool", "grp"), "cuts")),
        check_vma=False,
    )
```
